32 devices in a mesh: dp: 16 (over z, y, x), mp: 2 (over core).
Axes of the slice: x: 2, y: 2, z: 4, core: 2. Of those that a mesh axis runs over, the one named last changes fastest.
Arguments:
- short_input: bfloat16 [64, 128, 768], P('dp'), may hold values from -6 to 6
- long_input: bfloat16 [16, 512, 768], P('dp'), may hold values from -6 to 6
- query_weight: bfloat16 [768, 768], P(None, 'mp'), may hold values from -0.21875 to 0.21875
- query_bias: bfloat16 [768], P('mp'), may hold values from -3 to 3
- key_weight: bfloat16 [768, 768], P(None, 'mp'), may hold values from -0.21875 to 0.21875
- value_weight: bfloat16 [768, 768], P(None, 'mp'), may hold values from -0.21875 to 0.21875
- value_bias: bfloat16 [768], P('mp'), may hold values from -3 to 3
- output_weight: bfloat16 [768, 768], P('mp'), may hold values from -0.875 to 0.875
- output_bias: bfloat16 [768], replicated, may hold values from -3 to 3
- gain_one: bfloat16 [768], replicated, may hold values from 0.25 to 1.75
- shift_one: bfloat16 [768], replicated, may hold values from -2 to 2
- upward_weight: bfloat16 [768, 3072], P(None, 'mp'), may hold values from -0.21875 to 0.21875
- upward_bias: bfloat16 [3072], P('mp'), may hold values from -3 to 3
- downward_weight: bfloat16 [3072, 768], P('mp'), may hold values from -0.109375 to 0.109375
- downward_bias: bfloat16 [768], replicated, may hold values from -3 to 3
- gain_two: bfloat16 [768], replicated, may hold values from 0.25 to 1.75
- shift_two: bfloat16 [768], replicated, may hold values from -2 to 2
- short_upstream: bfloat16 [64, 128, 768], P('dp'), may hold values from -6 to 6
- long_upstream: bfloat16 [16, 512, 768], P('dp'), may hold values from -6 to 6
- short_lengths: int32 [64], P('dp'), may hold values from 64 to 128, as said below
- long_lengths: int32 [16], P('dp'), may hold values from 256 to 512, as said below
- live_counts: int32 [16, 2], P('dp'), may hold values from 0 to 4, as said below
Outputs:
- short_output: bfloat16 [64, 128, 768], P('dp')
- long_output: bfloat16 [16, 512, 768], P('dp')
- short_inputgrad: bfloat16 [64, 128, 768], P('dp')
- long_inputgrad: bfloat16 [16, 512, 768], P('dp')
- query_grad: float32 [768, 768], P('dp', 'mp')
- querybias_grad: float32 [768], P(('mp', 'dp'))
- key_grad: float32 [768, 768], P('dp', 'mp')
- value_grad: float32 [768, 768], P('dp', 'mp')
- valuebias_grad: float32 [768], P(('mp', 'dp'))
- output_grad: float32 [768, 768], P('mp', 'dp')
- outbias_grad: float32 [768], P('dp')
- gainone_grad: float32 [768], P('dp')
- shiftone_grad: float32 [768], P('dp')
- upward_grad: float32 [768, 3072], P('dp', 'mp')
- upbias_grad: float32 [3072], P(('mp', 'dp'))
- downward_grad: float32 [3072, 768], P('mp', 'dp')
- downbias_grad: float32 [768], P('dp')
- gaintwo_grad: float32 [768], P('dp')
- shifttwo_grad: float32 [768], P('dp')
The draws below stay inside these ranges and needn't reach their ends.
Inputs may be any that keep to these rules, and one draw needn't show every extreme that they name: `short_lengths`: in every draw some short slot holds 128 tokens and some holds 64. `long_lengths`: in every draw some long slot holds 512 tokens and some holds 256. `live_counts`: column 0 counts a device's live short slots, 2 to 4; column 1 its live long slots, 0 or 1; the live slots are a device's first ones; in every draw some device has all slots live and another has the fewest of both kinds.
All inputs are finite; a program needn't handle non-finite values.
Results may differ from the reference program's by a relative error of at most 0.02.
Values may be sent and summed in bfloat16 or wider, within the bound.
A program may use at most 128 MiB of HBM per device.

```python
import math
import jax
import jax.numpy as jnp
from jax import lax

D = 768
HEADS = 12
HEAD = 64
FF = 3072
SHORT_LEN = 128
LONG_LEN = 512
SHORT_DEV = 4
LONG_DEV = 1
SHORTS = 64
LONGS = 16
N_DP = 16


def picked_devices(key):
    key = jax.random.fold_in(key, 977)
    first_key, second_key = jax.random.split(key)
    fullest = jax.random.randint(first_key, (), 0, N_DP)
    fewest = (fullest + 1 + jax.random.randint(second_key, (), 0, N_DP - 1)) % N_DP
    return (fullest, fewest)


def draw_live_counts(key, part):
    fullest, fewest = picked_devices(key)
    key = jax.random.fold_in(key, 11)
    first_key, second_key = jax.random.split(key)
    short_live = SHORT_DEV - jax.random.randint(first_key, (N_DP,), 0, SHORT_DEV // 2 + 1)
    long_live = LONG_DEV - (jax.random.randint(second_key, (N_DP,), 0, 4) == 0).astype(jnp.int32)
    short_live = short_live.at[fullest].set(SHORT_DEV).at[fewest].set(SHORT_DEV - SHORT_DEV // 2)
    long_live = long_live.at[fullest].set(LONG_DEV).at[fewest].set(LONG_DEV - 1)
    return jnp.stack([short_live, long_live], axis=1).astype(jnp.int32)


def draw_short_lengths(key, part):
    fullest, fewest = picked_devices(key)
    key = jax.random.fold_in(key, 21)
    lengths = jax.random.randint(key, (SHORTS,), SHORT_LEN // 2, SHORT_LEN + 1)
    lengths = lengths.at[fullest * SHORT_DEV].set(SHORT_LEN).at[fewest * SHORT_DEV].set(SHORT_LEN // 2)
    return lengths.astype(jnp.int32)


def draw_long_lengths(key, part):
    fullest, fewest = picked_devices(key)
    key = jax.random.fold_in(key, 31)
    lengths = jax.random.randint(key, (LONGS,), LONG_LEN // 2, LONG_LEN + 1)
    lengths = lengths.at[fullest * LONG_DEV].set(LONG_LEN).at[fewest * LONG_DEV].set(LONG_LEN // 2)
    return lengths.astype(jnp.int32)


def strengthened(array, stream_key, source, target, parts, factor):
    def block_of(dim):
        return (jnp.arange(array.shape[dim]) // (array.shape[dim] // parts)).reshape((-1,) + (1,) * (array.ndim - 1 - dim))

    first = jax.random.permutation(stream_key, parts)[block_of(target)]
    second = (block_of(target) + parts // 2) % parts
    return jnp.where((block_of(source) == first) | (block_of(source) == second), factor * array, array)


def shard_levels(key, shape, pieces, smallest, largest):
    level, own = 1.0, jax.random.fold_in(key, 6)
    for dim, blocks in pieces:
        heights = jnp.exp(jax.random.uniform(jax.random.fold_in(own, dim), (blocks,), jnp.float32, smallest / len(pieces), largest / len(pieces)))
        level = level * jnp.repeat(heights, shape[dim] // blocks).reshape([-1 if axis == dim else 1 for axis in range(len(shape))])
    return level


def noise(stream_key, extent, scale, reach, shards=(), kind=jnp.bfloat16):
    level = shard_levels(stream_key, extent, shards, -0.22, 0.18) if shards else 1.0
    drawn = jax.random.normal(stream_key, extent, jnp.float32) * scale * level
    return jnp.minimum(jnp.maximum(drawn, -reach), reach).astype(kind)


def bell_draw_with(rng, shape, scale, bound, cuts, heavy, kind=jnp.bfloat16):
    entries = scale * jax.random.normal(rng, shape, jnp.float32)
    if cuts:
        entries = entries * shard_levels(rng, shape, cuts, -0.22, 0.18)
    return jnp.clip(strengthened(entries, jax.random.fold_in(rng, 3), *heavy), -bound, bound).astype(kind)


def setup_inputs(seed: int = 0) -> dict:
    streams_of = jax.random.split(jax.random.key(seed), 23)
    return {
        "short_input": noise(streams_of[0], (SHORTS, SHORT_LEN, D), 1.0, 6.0, ((0, 16),)),
        "long_input": noise(streams_of[1], (LONGS, LONG_LEN, D), 1.0, 6.0, ((0, 16),)),
        "query_weight": noise(streams_of[2], (D, D), D ** -0.5, 0.21875, ((1, 2),)),
        "query_bias": noise(streams_of[3], (D,), 0.5, 3.0, ((0, 2),)),
        "key_weight": noise(streams_of[4], (D, D), D ** -0.5, 0.21875, ((1, 2),)),
        "value_weight": noise(streams_of[5], (D, D), D ** -0.5, 0.21875, ((1, 2),)),
        "value_bias": noise(streams_of[6], (D,), 0.5, 3.0, ((0, 2),)),
        "output_weight": noise(streams_of[7], (D, D), (D // 16) ** -0.5, 0.875, ((0, 2),)),
        "output_bias": noise(streams_of[8], (D,), 0.5, 3.0),
        "gain_one": jnp.clip(1.0 + 0.15 * jax.random.normal(streams_of[9], (D,), jnp.float32), 0.25, 1.75).astype(jnp.bfloat16),
        "shift_one": noise(streams_of[10], (D,), 0.3, 2.0),
        "upward_weight": noise(streams_of[11], (D, FF), D ** -0.5, 0.21875, ((1, 2),)),
        "upward_bias": noise(streams_of[12], (FF,), 0.5, 3.0, ((0, 2),)),
        "downward_weight": noise(streams_of[13], (FF, D), FF ** -0.5, 0.109375, ((0, 2),)),
        "downward_bias": noise(streams_of[14], (D,), 0.5, 3.0),
        "gain_two": jnp.clip(1.0 + 0.15 * jax.random.normal(streams_of[15], (D,), jnp.float32), 0.25, 1.75).astype(jnp.bfloat16),
        "shift_two": noise(streams_of[16], (D,), 0.3, 2.0),
        "short_upstream": bell_draw_with(streams_of[17], (SHORTS, SHORT_LEN, D), 1.0, 6.0, ((0, 16),), (0, 2, 16, 2.0)),
        "long_upstream": bell_draw_with(streams_of[18], (LONGS, LONG_LEN, D), 1.0, 6.0, ((0, 16),), (0, 2, 16, 2.0)),
        "short_lengths": draw_short_lengths(jax.random.fold_in(streams_of[22], 71), 0),
        "long_lengths": draw_long_lengths(jax.random.fold_in(streams_of[22], 71), 0),
        "live_counts": draw_live_counts(jax.random.fold_in(streams_of[22], 71), 0),
    }


@jax.custom_vjp
def low(v):
    return lax.optimization_barrier(v.astype(jnp.bfloat16)).astype(jnp.float32)

@jax.custom_vjp
def low_back(v):
    return v

def low_keep(v):
    return (low(v), None)

def low_pass(kept, grad):
    return (grad,)

def back_keep(v):
    return (v, None)

def back_low(kept, grad):
    return (low(grad),)
low.defvjp(low_keep, low_pass)
low_back.defvjp(back_keep, back_low)
NEGATIVE = -1e+30

def product(left, right):
    return jnp.dot(left, right, precision=lax.Precision.HIGHEST, preferred_element_type=jnp.float32)

def layer_norm(values, gain, shift):
    mean = lax.optimization_barrier(jnp.mean(values, axis=-1, keepdims=True))
    centred = values - mean
    spread = lax.optimization_barrier(jnp.mean(centred * centred, axis=-1, keepdims=True))
    return centred * lax.rsqrt(spread + 1e-12) * gain + shift

def slot_keep(lengths, live, per_device, length):
    slots = lengths.shape[0]
    slot_index = jnp.arange(slots, dtype=jnp.int32)
    owner = slot_index // per_device
    alive = slot_index % per_device < live[owner]
    position = jnp.arange(length, dtype=jnp.int32)
    keep = (position[None, :] < lengths[:, None]) & alive[:, None]
    return keep.astype(jnp.float32)

def layer(params, inputs, keep):
    query_weight, query_bias, key_weight, value_weight, value_bias, output_weight, output_bias, gain_one, shift_one, upward_weight, upward_bias, downward_weight, downward_bias, gain_two, shift_two = params
    group, length, width = inputs.shape
    flat = inputs.reshape(group * length, width)

    def split_heads(matrix):
        return matrix.reshape(group, length, HEADS, HEAD)
    query = split_heads(low(low_back(product(flat, query_weight) + query_bias)))
    keyed = split_heads(low(low_back(product(flat, key_weight))))
    valued = split_heads(low(low_back(product(flat, value_weight) + value_bias)))
    scores = jnp.einsum('gqhd,gkhd->ghqk', query, keyed, precision=lax.Precision.HIGHEST) * HEAD ** (-0.5)
    scores = low_back(jnp.where(keep[:, None, None, :] > 0, scores, NEGATIVE))
    probs = low(jax.nn.softmax(scores, axis=-1))
    context = jnp.einsum('ghqk,gkhd->gqhd', probs, valued, precision=lax.Precision.HIGHEST)
    context = low(low_back(context)).reshape(group * length, width)
    attended = low_back(product(context, output_weight) + output_bias)
    hidden = layer_norm(flat + attended, gain_one, shift_one)
    pre = low_back(product(low(hidden), upward_weight) + upward_bias)
    active = low(jax.nn.gelu(pre, approximate=False))
    fed = low_back(product(active, downward_weight) + downward_bias)
    result = layer_norm(hidden + fed, gain_two, shift_two) * keep.reshape(-1)[:, None]
    return result.reshape(group, length, width)

def bucket(params, inputs, keep):
    slots, length, width = inputs.shape
    group = math.gcd(slots, max(1, 4096 // length))
    grouped = inputs.reshape(slots // group, group, length, width)
    keep_grouped = keep.reshape(slots // group, group, length)
    step = jax.checkpoint(lambda pair: layer(params, pair[0], pair[1]))
    result = lax.map(step, (grouped, keep_grouped))
    return result.reshape(slots, length, width)

def reference(short_input, long_input, query_weight, query_bias, key_weight, value_weight, value_bias, output_weight, output_bias, gain_one, shift_one, upward_weight, upward_bias, downward_weight, downward_bias, gain_two, shift_two, short_upstream, long_upstream, short_lengths, long_lengths, live_counts):
    params = tuple((item.astype(jnp.float32) for item in (query_weight, query_bias, key_weight, value_weight, value_bias, output_weight, output_bias, gain_one, shift_one, upward_weight, upward_bias, downward_weight, downward_bias, gain_two, shift_two)))
    keep_short = slot_keep(short_lengths, live_counts[:, 0], SHORT_DEV, SHORT_LEN)
    keep_long = slot_keep(long_lengths, live_counts[:, 1], LONG_DEV, LONG_LEN)

    def forward(weights, short_wide, long_wide):
        return (bucket(weights, short_wide, keep_short), bucket(weights, long_wide, keep_long))
    outputs, backward = jax.vjp(forward, params, short_input.astype(jnp.float32), long_input.astype(jnp.float32))
    grads, short_grad, long_grad = backward((short_upstream.astype(jnp.float32), long_upstream.astype(jnp.float32)))
    return (outputs[0].astype(jnp.bfloat16), outputs[1].astype(jnp.bfloat16), short_grad.astype(jnp.bfloat16), long_grad.astype(jnp.bfloat16), grads[0], grads[1], grads[2], grads[3], grads[4], grads[5], grads[6], grads[7], grads[8], grads[9], grads[10], grads[11], grads[12], grads[13], grads[14])
```

```python
import functools

import jax
import jax.numpy as jnp
from jax import lax
from jax.experimental import pallas as pl
from jax.experimental.pallas import tpu as pltpu
from jax.sharding import PartitionSpec as P

HEAD = 64
PAIR = 2 * HEAD
NEGATIVE = -1e30
EPSILON = 1e-12
BF = jnp.bfloat16
F32 = jnp.float32
MESH = pl.DeviceIdType.MESH

BITS = 4
X, Y, NEAR, FAR = 0, 1, 2, 3
ORDERS = ((X, Y, NEAR, FAR), (Y, NEAR, X, FAR), (NEAR, X, Y, FAR))
KINDS = (0, 1, 2, 0, 1, 2, 0, 1, 2, 0, 1, 0)
PARTS_AT = (0, 8, 12, 14)


def mm(left, right):
    return jnp.dot(left, right, preferred_element_type=F32)


def mm_nt(left, right):
    return lax.dot_general(left, right, (((1,), (1,)), ((), ())), preferred_element_type=F32)


def mm_tn(left, right):
    return lax.dot_general(left, right, (((0,), (0,)), ((), ())), preferred_element_type=F32)


def rows_of(start, size):
    return pl.ds(pl.multiple_of(start, size), size)


def fold(values):
    rows, width = values.shape
    return jnp.sum(values.reshape(rows // 8, 8, width), axis=0)


def place(order, block):
    spot = 0
    for bit in order:
        spot = spot * 2 + ((block >> bit) & 1)
    return spot


class Refs:
    pass


def layer(reduce_here, names, *refs):
    r = Refs()
    for name, ref in zip(names, refs, strict=True):
        setattr(r, name, ref)
    dp, mp = lax.axis_index("dp"), lax.axis_index("mp")
    peer = (dp, 1 - mp)
    half = r.own.shape[1]
    seg_rows = 2 * half
    width = r.x.shape[1]
    local = r.q.shape[1]
    pairs = local // PAIR
    hidden = r.f.shape[1]
    short_slots, short_length = r.xs.shape[0], r.xs.shape[1]
    long_length = r.xl.shape[1]
    chunk = r.G.shape[3]
    block = r.G.shape[2]
    tile = 64

    my_bit = [lax.rem(lax.div(dp, 1 << k), 2) for k in range(BITS)]
    across = [(dp + (1 - 2 * my_bit[k]) * (1 << k), mp) for k in range(BITS)]

    loads = {}

    def load(name, src, dst):
        cp = pltpu.make_async_copy(src, dst, r.load_sem.at[len(loads)])
        cp.start()
        loads[name] = cp

    load("xl", r.xl.at[0], r.x.at[pl.ds(seg_rows, seg_rows)])
    load("wq", r.wq_h, r.wq)
    load("wk", r.wk_h, r.wk)
    load("wv", r.wv_h, r.wv)
    for s in range(short_slots):
        load(f"xs{s}", r.xs.at[s], r.x.at[pl.ds(s * short_length, short_length)])
    load("wo", r.wo_h, r.wo)
    load("wu", r.wu_h, r.wu)
    load("wd", r.wd_h, r.wd)
    load("us", r.us.at[pl.ds(mp * (short_slots // 2), short_slots // 2)], r.ups)
    load("ul", r.ul.at[0, rows_of(mp * half, half)], r.upl)

    barrier = pltpu.get_barrier_semaphore()
    partners = [peer] + (across if reduce_here else [])
    for other in partners:
        pl.semaphore_signal(barrier, inc=1, device_id=other, device_id_type=MESH)

    sends = []

    def remote(src, dst, index, device):
        cp = pltpu.make_async_remote_copy(
            src_ref=src,
            dst_ref=dst,
            send_sem=r.ex_send.at[index],
            recv_sem=r.ex_recv.at[index],
            device_id=device,
            device_id_type=MESH,
        )
        cp.start()
        sends.append(cp)
        return cp

    live_short, live_long = r.live[0, 0], r.live[0, 1]
    long_len = jnp.where(live_long > 0, r.ll[0], 0)

    def short_len(slot):
        return jnp.where(slot < live_short, r.sl[slot], 0)

    def param(ref):
        return ref[...].astype(F32).reshape(1, -1)

    qb, vb, ob, g1, b1 = (param(n) for n in (r.qb, r.vb, r.ob, r.g1, r.b1))
    ub, db, g2, b2 = (param(n) for n in (r.ub, r.db, r.g2, r.b2))

    low_lane = lax.broadcasted_iota(jnp.int32, (1, PAIR), 1) < HEAD

    def first(values):
        return jnp.where(low_lane, values, jnp.zeros_like(values))

    def second(values):
        return jnp.where(low_lane, jnp.zeros_like(values), values)

    def own_start(seg):
        return seg * seg_rows + mp * half

    def peer_start(seg):
        return seg * seg_rows + (1 - mp) * half

    r.acc[...] = jnp.zeros_like(r.acc)
    r.acc_up[...] = jnp.zeros_like(r.acc_up)
    r.acc_qv[...] = jnp.zeros_like(r.acc_qv)

    def project(seg):
        rows = slice(seg * seg_rows, (seg + 1) * seg_rows)
        tokens = r.x[rows, :]
        r.q[rows, :] = (mm(tokens, r.wq[...]) + qb).astype(BF) * BF(HEAD**-0.5)
        r.k[rows, :] = mm(tokens, r.wk[...]).astype(BF)
        r.v[rows, :] = (mm(tokens, r.wv[...]) + vb).astype(BF)

    def softmax(scores):
        highest = jnp.max(scores, axis=-1, keepdims=True)
        expo = jnp.exp(scores - highest)
        total = jnp.sum(expo, axis=-1, keepdims=True)
        return (expo * (1.0 / total)).astype(BF)

    def attend(rows, keys, bias, pair, store):
        lanes = slice(pair * PAIR, (pair + 1) * PAIR)
        qp, kp, vp = r.q[rows, lanes], r.k[keys, lanes], r.v[keys, lanes]
        p0 = softmax(mm_nt(first(qp), kp) + bias)
        p1 = softmax(mm_nt(second(qp), kp) + bias)
        store(2 * pair, p0)
        store(2 * pair + 1, p1)
        r.ctx[rows, lanes] = jnp.where(low_lane, mm(p0, vp), mm(p1, vp)).astype(BF)

    def attend_long():
        tq = 128
        position = lax.broadcasted_iota(jnp.int32, (1, long_length), 1)
        bias = jnp.where(position < long_len, 0.0, NEGATIVE)
        keys = slice(seg_rows, 2 * seg_rows)

        @pl.loop(0, long_length // tq)
        def _(t):
            def store(head, probs):
                r.pl[head, rows_of(t * tq, tq), :] = probs

            for pair in range(pairs):
                attend(rows_of(seg_rows + t * tq, tq), keys, bias, pair, store)

    def attend_short():
        position = lax.broadcasted_iota(jnp.int32, (1, short_length), 1)

        @pl.loop(0, short_slots)
        def _(s):
            bias = jnp.where(position < short_len(s), 0.0, NEGATIVE)
            rows = rows_of(s * short_length, short_length)

            def store(head, probs):
                r.ps[s, head] = probs

            for pair in range(pairs):
                attend(rows, rows, bias, pair, store)

    def exchange(stage, seg, left, right, product):
        index = 2 * stage + seg
        r.out_buf[index] = product(left[rows_of(peer_start(seg), half), :], right[...]).astype(BF)
        cp = remote(r.out_buf.at[index], r.in_buf.at[index], index, peer)
        r.own[seg] = product(left[rows_of(own_start(seg), half), :], right[...])
        return cp

    def share(index, seg, ref):
        rows = rows_of(own_start(seg), half)
        return remote(ref.at[rows], ref.at[rows], index, peer)

    def norm(values):
        mean = jnp.mean(values, axis=-1, keepdims=True)
        centred = values - mean
        scale = lax.rsqrt(jnp.mean(centred * centred, axis=-1, keepdims=True) + EPSILON)
        return centred * scale, scale

    def norm_back(normed, scale, grad):
        return scale * (
            grad
            - jnp.mean(grad, axis=-1, keepdims=True)
            - normed * jnp.mean(grad * normed, axis=-1, keepdims=True)
        )

    def norm_one(seg):
        @pl.loop(0, half // tile)
        def _(t):
            mine = rows_of(seg * half + t * tile, tile)
            here = rows_of(t * tile, tile)
            rows = rows_of(own_start(seg) + t * tile, tile)
            total = r.own[seg, here, :] + r.in_buf[seg, here, :].astype(F32) + ob
            normed, scale = norm(r.x[rows, :].astype(F32) + total)
            r.n1[mine, :] = normed
            r.r1[mine, :] = scale
            r.h[rows, :] = (normed * g1 + b1).astype(BF)

    def up(start):
        rows = rows_of(start, half)
        step = 512
        for j in range(hidden // step):
            cols = slice(j * step, (j + 1) * step)
            pre = mm(r.h[rows, :], r.wu[:, cols]) + ub[:, cols]
            phi = 0.5 + 0.5 * lax.erf(pre * (0.5**0.5))
            r.f[rows, cols] = (pre * phi).astype(BF)
            r.gp[rows, cols] = (phi + pre * (jnp.exp(pre * pre * -0.5) * 0.3989422804014327)).astype(BF)

    def norm_two(seg):
        @pl.loop(0, half // tile)
        def _(t):
            mine = rows_of(seg * half + t * tile, tile)
            here = rows_of(t * tile, tile)
            rows = rows_of(own_start(seg) + t * tile, tile)
            row = lax.broadcasted_iota(jnp.int32, (tile, 1), 0)
            if seg == 0:
                per_slot = short_length // tile
                slot = lax.div(t, per_slot)
                inner = rows_of(lax.rem(t, per_slot) * tile, tile)
                keep = row + lax.rem(t, per_slot) * tile < short_len(mp * (short_slots // 2) + slot)
                upstream = r.ups[slot, inner, :]
            else:
                keep = row + (mp * half + t * tile) < long_len
                upstream = r.upl[here, :]
            keep = keep.astype(F32)
            hidden_state = r.n1[mine, :] * g1 + b1
            total = r.own[seg, here, :] + r.in_buf[2 + seg, here, :].astype(F32) + db
            normed, scale = norm(hidden_state + total)
            r.out[seg, here, :] = (keep * (normed * g2 + b2)).astype(BF)
            grad = keep * upstream.astype(F32)
            r.acc[0] += fold(grad * normed)
            r.acc[1] += fold(grad)
            dsecond = norm_back(normed, scale, grad * g2)
            low = dsecond.astype(BF)
            r.acc[2] += fold(low.astype(F32))
            r.ds[mine, :] = dsecond
            r.do[rows, :] = low

    def norm_one_back(seg):
        @pl.loop(0, half // tile)
        def _(t):
            mine = rows_of(seg * half + t * tile, tile)
            here = rows_of(t * tile, tile)
            rows = rows_of(own_start(seg) + t * tile, tile)
            grad = r.ds[mine, :] + r.own[seg, here, :] + r.in_buf[4 + seg, here, :].astype(F32)
            normed = r.n1[mine, :]
            r.acc[3] += fold(grad * normed)
            r.acc[4] += fold(grad)
            dfirst = norm_back(normed, r.r1[mine, :], grad * g1)
            low = dfirst.astype(BF)
            r.acc[5] += fold(low.astype(F32))
            r.ds[mine, :] = dfirst
            r.da[rows, :] = low

    def active_back(seg):
        for part in range(2):
            rows = slice(seg * seg_rows + part * half, seg * seg_rows + (part + 1) * half)
            step = 512
            for j in range(hidden // step):
                cols = slice(j * step, (j + 1) * step)
                low = (mm_nt(r.do[rows, :], r.wd[cols, :]) * r.gp[rows, cols].astype(F32)).astype(BF)
                r.acc_up[:, cols] += fold(low.astype(F32))
                r.gp[rows, cols] = low

    def attend_back(rows, keys, pair, probs, dscores):
        lanes = slice(pair * PAIR, (pair + 1) * PAIR)
        kp, vp, dc = r.k[keys, lanes], r.v[keys, lanes], r.dctx[rows, lanes]
        product = dc.astype(F32) * r.ctx[rows, lanes].astype(F32)
        parts = []
        for j, pick in enumerate((first, second)):
            inner = jnp.sum(pick(product), axis=-1, keepdims=True)
            low = (probs(2 * pair + j).astype(F32) * (mm_nt(pick(dc), vp) - inner)).astype(BF)
            dscores(j, low)
            parts.append(mm(low, kp))
        dq = (jnp.where(low_lane, parts[0], parts[1]) * HEAD**-0.5).astype(BF)
        r.dq[rows, lanes] = dq

    def keys_back(rows, pair, probs, dscores):
        lanes = slice(pair * PAIR, (pair + 1) * PAIR)
        qp, dc = r.q[rows, lanes], r.dctx[rows, lanes]
        r.dk[rows, lanes] = jnp.where(low_lane, mm_tn(dscores(0), qp), mm_tn(dscores(1), qp)).astype(BF)
        dv = jnp.where(low_lane, mm_tn(probs(2 * pair), dc), mm_tn(probs(2 * pair + 1), dc))
        r.dv[rows, lanes] = dv.astype(BF)

    def attend_long_back():
        tq = 128
        keys = slice(seg_rows, 2 * seg_rows)
        for pair in range(pairs):

            @pl.loop(0, long_length // tq)
            def _(t, pair=pair):
                here = rows_of(t * tq, tq)

                def store(j, low):
                    r.dS[j, here, :] = low

                attend_back(rows_of(seg_rows + t * tq, tq), keys, pair, lambda head: r.pl[head, here, :], store)

            keys_back(keys, pair, lambda head: r.pl[head], lambda j: r.dS[j])

    def attend_short_back():
        @pl.loop(0, short_slots)
        def _(s):
            rows = rows_of(s * short_length, short_length)
            for pair in range(pairs):
                held = [None, None]

                def store(j, low, held=held):
                    held[j] = low

                attend_back(rows, rows, pair, lambda head: r.ps[s, head], store)
                keys_back(rows, pair, lambda head: r.ps[s, head], lambda j, held=held: held[j])

    begin = {}

    def half_copy(c, p):
        order = ORDERS[KINDS[c]]
        if p == 0:
            begin[c] = 0
        n = 8 >> p
        bit = order[p]
        cp = pltpu.make_async_remote_copy(
            src_ref=r.G.at[c, pl.ds(begin[c] + (1 - my_bit[bit]) * n, n)],
            dst_ref=r.R.at[c, pl.ds(PARTS_AT[p], n)],
            send_sem=r.rs_send.at[c, p],
            recv_sem=r.rs_recv.at[c, p],
            device_id=across[bit],
            device_id_type=MESH,
        )
        cp.start()
        sends.append(cp)
        begin[c] = begin[c] + my_bit[bit] * n
        flight[c] = (p, cp)

    flight = {}

    def gradient(c, left, right):
        order = ORDERS[KINDS[c]] if reduce_here else (3, 2, 1, 0)
        blocks = width // block
        for m in range(2):
            part = width // 2
            piece = mm_tn(left[:, m * part : (m + 1) * part], right).astype(BF)
            for b in range(blocks // 2):
                r.G[c, place(order, m * blocks // 2 + b)] = piece[b * block : (b + 1) * block]
        if reduce_here:
            half_copy(c, 0)

    def advance(c):
        p, cp = flight[c]
        n = 8 >> p
        cp.wait_recv()
        if p < BITS - 1:
            mine = pl.ds(begin[c], n)
            r.G[c, mine] = r.G[c, mine] + r.R[c, PARTS_AT[p] : PARTS_AT[p] + n]
            half_copy(c, p + 1)
        else:
            total = r.G[c, begin[c]].astype(F32) + r.R[c, PARTS_AT[p]].astype(F32)
            ref, at, turned = r.targets[c]
            if turned:
                ref[at * chunk : (at + 1) * chunk, :] = total.T
            else:
                ref[:, at * chunk : (at + 1) * chunk] = total

    ups = hidden // chunk
    if reduce_here:
        r.targets = (
            [(r.gdown, j, True) for j in range(ups)]
            + [(r.gup, j, False) for j in range(ups)]
            + [(r.gout, 0, True), (r.gq, 0, False), (r.gk, 0, False), (r.gv, 0, False)]
        )
    todo = list(EVENTS) if reduce_here else []

    def drain(upto):
        while todo and len(EVENTS) - len(todo) < upto:
            advance(todo.pop(0))

    for name in ("xl", "wq", "wk", "wv"):
        loads[name].wait()
    project(1)
    attend_long()
    for s in range(short_slots):
        loads[f"xs{s}"].wait()
    loads["wo"].wait()
    pl.semaphore_wait(barrier, len(partners))
    ex = {}
    ex["a1"] = exchange(0, 1, r.ctx, r.wo, mm)
    project(0)
    attend_short()
    ex["a0"] = exchange(0, 0, r.ctx, r.wo, mm)
    loads["wu"].wait()
    loads["wd"].wait()
    ex["a1"].wait_recv()
    norm_one(1)
    ex["h1"] = share(8, 1, r.h)
    ex["a0"].wait_recv()
    norm_one(0)
    ex["h0"] = share(9, 0, r.h)
    for seg in (1, 0):
        up(own_start(seg))
        ex[f"h{seg}"].wait_recv()
        up(peer_start(seg))
        ex[f"o{seg}"] = exchange(1, seg, r.f, r.wd, mm)
    loads["us"].wait()
    loads["ul"].wait()
    outs, arrivals = [], []

    def publish(index, seg, short_ref, long_ref, held):
        if seg == 0:
            for s in range(short_slots // 2):
                piece = held.at[0, pl.ds(s * short_length, short_length)]
                target = short_ref.at[mp * (short_slots // 2) + s]
                cp = pltpu.make_async_copy(piece, target, r.out_sem.at[index + s])
                cp.start()
                outs.append(cp)
                arrivals.append(remote(piece, target, 16 + index + s, peer))
        else:
            target = long_ref.at[0, rows_of(mp * half, half)]
            cp = pltpu.make_async_copy(held.at[1], target, r.out_sem.at[index + 2])
            cp.start()
            outs.append(cp)
            arrivals.append(remote(held.at[1], target, 16 + index + 2, peer))

    for seg in (1, 0):
        ex[f"o{seg}"].wait_recv()
        norm_two(seg)
        ex[f"do{seg}"] = share(10 + seg, seg, r.do)
    ex["do1"].wait_recv()
    ex["do0"].wait_recv()

    for j in range(ups):
        gradient(j, r.do, r.f[:, j * chunk : (j + 1) * chunk])
    publish(0, 1, r.os, r.ol, r.out)
    publish(0, 0, r.os, r.ol, r.out)
    active_back(1)
    drain(MARKS[0])
    active_back(0)
    drain(MARKS[1])
    for j in range(ups):
        gradient(ups + j, r.h, r.gp[:, j * chunk : (j + 1) * chunk])
    drain(MARKS[2])
    for seg in (1, 0):
        ex[f"dh{seg}"] = exchange(2, seg, r.gp, r.wu, mm_nt)
    drain(MARKS[3])
    for seg in (1, 0):
        ex[f"dh{seg}"].wait_recv()
        norm_one_back(seg)
        ex[f"da{seg}"] = share(12 + seg, seg, r.da)
    drain(MARKS[4])
    for seg in (1, 0):
        ex[f"da{seg}"].wait_recv()
        rows = slice(seg * seg_rows, (seg + 1) * seg_rows)
        r.dctx[rows, :] = mm_nt(r.da[rows, :], r.wo[...]).astype(BF)
    gradient(2 * ups, r.da, r.ctx[...])
    drain(MARKS[5])
    attend_long_back()
    drain(MARKS[6])
    attend_short_back()
    drain(MARKS[7])
    for j, ref in enumerate((r.dq, r.dk, r.dv)):
        gradient(2 * ups + 1 + j, r.x, ref[...])
    r.acc_qv[:, :local] = fold(r.dq[...].astype(F32))
    r.acc_qv[:, local:] = fold(r.dv[...].astype(F32))
    drain(MARKS[8])

    def total_of(values):
        return jnp.sum(values, axis=0, keepdims=True)

    r.vec[...] = jnp.zeros_like(r.vec)
    r.vec[0:1, :] = total_of(r.acc_qv[...])
    r.vec[1:2, :] = total_of(r.acc_up[:, :width])
    r.vec[2:3, :] = total_of(r.acc_up[:, width:])
    for j in range(6):
        r.vec[8 + j : 9 + j, :] = total_of(r.acc[j])
    r.vec_out[0] = r.vec[...]
    vec_copy = remote(r.vec_out.at[0, pl.ds(8, 8)], r.vec_in.at[0, pl.ds(8, 8)], 14, peer)

    def input_part(rows):
        return (
            mm_nt(r.dq[rows, :], r.wq[...])
            + mm_nt(r.dk[rows, :], r.wk[...])
            + mm_nt(r.dv[rows, :], r.wv[...])
        )

    for seg in (1, 0):
        index = 6 + seg
        r.out_buf[index] = input_part(rows_of(peer_start(seg), half)).astype(BF)
        ex[f"dx{seg}"] = remote(r.out_buf.at[index], r.in_buf.at[index], index, peer)
        r.own[seg] = input_part(rows_of(own_start(seg), half))
    vec_copy.wait_recv()
    r.vec[8:16, :] = r.vec[8:16, :] + r.vec_in[0, 8:16, :]
    drain(MARKS[9])
    if reduce_here:
        r.vec_out[1] = r.vec[...]
        vec_copy = remote(r.vec_out.at[1], r.vec_in.at[1], 15, across[0])
    for seg in (1, 0):
        ex[f"dx{seg}"].wait_recv()
        dfirst = r.ds[seg * half : (seg + 1) * half, :]
        r.dxo[seg] = (dfirst + r.own[seg] + r.in_buf[6 + seg].astype(F32)).astype(BF)
        publish(3, seg, r.dxs, r.dxl, r.dxo)
    if reduce_here:
        drain(MARKS[10])
        for k in range(1, BITS + 1):
            vec_copy.wait_recv()
            r.vec[...] = r.vec[...] + r.vec_in[k]
            if k < BITS:
                r.vec_out[k + 1] = r.vec[...]
                vec_copy = remote(r.vec_out.at[k + 1], r.vec_in.at[k + 1], 21 + k, across[k])
            drain(MARKS[10 + k])
        high = r.vec[...].astype(BF)
        rest = r.vec[...] - high.astype(F32)
        middle = rest.astype(BF)
        last = (rest - middle.astype(F32)).astype(BF)

        def pick(size, offset):
            source = lax.broadcasted_iota(jnp.int32, (width, PAIR), 0)
            target = lax.broadcasted_iota(jnp.int32, (width, PAIR), 1)
            chosen = (source - target == dp * size + offset) & (target < size)
            chosen = chosen.astype(BF)
            return mm(high, chosen) + mm(middle, chosen) + mm(last, chosen)

        shared = pick(block, 0)
        for j, ref in enumerate((r.g_gain2, r.g_shift2, r.g_db, r.g_gain1, r.g_shift1, r.g_ob)):
            ref[...] = shared[8 + j : 9 + j, :block]
        size = r.g_qb.shape[1]
        r.g_qb[...] = pick(size, 0)[0:1, :size]
        r.g_vb[...] = pick(size, local)[0:1, :size]
        size = r.g_ub.shape[1]
        r.g_ub[...] = (pick(size, 0)[1:2, :] + pick(size, -width)[2:3, :])[:, :size]
        drain(len(EVENTS))
    else:
        r.vec_part[...] = r.vec[...]
        cp = pltpu.make_async_copy(r.G, r.grads, r.out_sem.at[6])
        cp.start()
        cp.wait()

    for cp in outs:
        cp.wait()
    for cp in arrivals:
        cp.wait_recv()
    for cp in sends:
        cp.wait_send()


EVENTS = tuple(c for wave in ((0, 1, 2), (3, 4, 5), (6, 7, 8), (9, 10, 11)) for p in range(BITS) for c in wave)
MARKS = (0, 3, 6, 9, 12, 18, 21, 24, 27, 30, 33, 36, 39, 42, 48)


def shards(n_dp, *args):
    (
        xs, xl, wq, qb, wk, wv, vb, wo, ob, g1, b1, wu, ub, wd, db, g2, b2, us, ul, sl, ll, live,
    ) = args
    short_slots, short_length, width = xs.shape
    long_length = xl.shape[1]
    local, hidden = wq.shape[1], wu.shape[1]
    heads = local // HEAD
    rows = short_slots * short_length + xl.shape[0] * long_length
    half = long_length // 2
    reduce_here = n_dp == 1 << BITS
    blocks = 1 << BITS
    block = width // blocks
    chunk = local
    chunks = (4 * local + 2 * hidden) // chunk
    any_spec = pl.BlockSpec(memory_space=pl.ANY)
    vmem = pl.BlockSpec(memory_space=pltpu.VMEM)
    smem = pl.BlockSpec(memory_space=pltpu.SMEM)
    inputs = [
        ("sl", sl, smem), ("ll", ll, smem), ("live", live, smem),
        ("xs", xs, any_spec), ("xl", xl, any_spec), ("us", us, any_spec), ("ul", ul, any_spec),
        ("wq_h", wq, any_spec), ("wk_h", wk, any_spec), ("wv_h", wv, any_spec), ("wo_h", wo, any_spec),
        ("wu_h", wu, any_spec), ("wd_h", wd, any_spec),
        ("qb", qb, vmem), ("vb", vb, vmem), ("ob", ob, vmem), ("g1", g1, vmem), ("b1", b1, vmem),
        ("ub", ub, vmem), ("db", db, vmem), ("g2", g2, vmem), ("b2", b2, vmem),
    ]
    sds = jax.ShapeDtypeStruct
    outputs = [
        ("os", sds(xs.shape, BF), any_spec), ("ol", sds(xl.shape, BF), any_spec),
        ("dxs", sds(xs.shape, BF), any_spec), ("dxl", sds(xl.shape, BF), any_spec),
    ]
    if reduce_here:
        for name, shape in (
            ("gq", (block, local)), ("gk", (block, local)), ("gv", (block, local)), ("gout", (local, block)),
            ("gup", (block, hidden)), ("gdown", (hidden, block)),
            ("g_qb", (1, local // blocks)), ("g_vb", (1, local // blocks)), ("g_ub", (1, hidden // blocks)),
            ("g_ob", (1, block)), ("g_gain1", (1, block)), ("g_shift1", (1, block)),
            ("g_db", (1, block)), ("g_gain2", (1, block)), ("g_shift2", (1, block)),
        ):
            outputs.append((name, sds(shape, F32), vmem))
    else:
        outputs.append(("grads", sds((chunks, blocks, block, chunk), BF), any_spec))
        outputs.append(("vec_part", sds((16, width), F32), vmem))
    v = pltpu.VMEM
    dma = pltpu.SemaphoreType.DMA
    scratch = [
        ("x", v((rows, width), BF)), ("ups", v((short_slots // 2, short_length, width), BF)), ("upl", v((half, width), BF)),
        ("wq", v(wq.shape, BF)), ("wk", v(wk.shape, BF)), ("wv", v(wv.shape, BF)), ("wo", v(wo.shape, BF)),
        ("wu", v(wu.shape, BF)), ("wd", v(wd.shape, BF)),
        ("q", v((rows, local), BF)), ("k", v((rows, local), BF)), ("v", v((rows, local), BF)),
        ("pl", v((heads, long_length, long_length), BF)), ("ps", v((short_slots, heads, short_length, short_length), BF)),
        ("ctx", v((rows, local), BF)), ("n1", v((2 * half, width), F32)), ("r1", v((2 * half, 1), F32)),
        ("h", v((rows, width), BF)), ("f", v((rows, hidden), BF)), ("gp", v((rows, hidden), BF)),
        ("do", v((rows, width), BF)), ("ds", v((2 * half, width), F32)), ("da", v((rows, width), BF)),
        ("dctx", v((rows, local), BF)), ("dq", v((rows, local), BF)), ("dk", v((rows, local), BF)), ("dv", v((rows, local), BF)),
        ("dS", v((2, long_length, long_length), BF)),
        ("G", v((chunks, blocks, block, chunk), BF)), ("R", v((chunks if reduce_here else 1, blocks - 1, block, chunk), BF)),
        ("own", v((2, half, width), F32)), ("out_buf", v((8, half, width), BF)), ("in_buf", v((8, half, width), BF)),
        ("out", v((2, half, width), BF)), ("dxo", v((2, half, width), BF)),
        ("acc", v((6, 8, width), F32)), ("acc_up", v((8, hidden), F32)), ("acc_qv", v((8, 2 * local), F32)),
        ("vec", v((16, width), F32)), ("vec_out", v((5, 16, width), F32)), ("vec_in", v((5, 16, width), F32)),
        ("load_sem", dma((16,))), ("out_sem", dma((8,))), ("ex_send", dma((28,))), ("ex_recv", dma((28,))),
        ("rs_send", dma((chunks, BITS))), ("rs_recv", dma((chunks, BITS))),
    ]
    names = [n for n, *_ in inputs] + [n for n, *_ in outputs] + [n for n, *_ in scratch]
    macs = rows * width * (8 * local + 6 * hidden)
    results = pl.pallas_call(
        functools.partial(layer, reduce_here, names),
        out_shape=[o[1] for o in outputs],
        in_specs=[i[2] for i in inputs],
        out_specs=[o[2] for o in outputs],
        scratch_shapes=[s[1] for s in scratch],
        cost_estimate=pl.CostEstimate(flops=2 * macs, bytes_accessed=20 << 20, transcendentals=0),
        compiler_params=pltpu.CompilerParams(
            collective_id=0, has_side_effects=True, vmem_limit_bytes=62 << 20
        ),
    )(*[i[1] for i in inputs])
    got = dict(zip([o[0] for o in outputs], results, strict=True))
    if not reduce_here:
        n = n_dp
        grads = got["grads"].reshape(chunks, width, chunk).astype(F32)
        grads = lax.psum_scatter(grads, "dp", scatter_dimension=1, tiled=True)
        vec = lax.psum(got["vec_part"], "dp")
        at = lax.axis_index("dp")
        ups = hidden // chunk
        wide = grads.transpose(1, 0, 2)
        got["gdown"] = wide[:, :ups].reshape(width // n, hidden).T
        got["gup"] = wide[:, ups : 2 * ups].reshape(width // n, hidden)
        got["gout"] = grads[2 * ups].T
        got["gq"], got["gk"], got["gv"] = grads[2 * ups + 1], grads[2 * ups + 2], grads[2 * ups + 3]

        def mine(values):
            size = values.shape[0] // n
            return lax.dynamic_slice(values, (at * size,), (size,))

        got["g_qb"], got["g_vb"] = mine(vec[0, :local]), mine(vec[0, local:])
        got["g_ub"] = mine(vec[1:3].reshape(-1))
        for j, name in enumerate(("g_gain2", "g_shift2", "g_db", "g_gain1", "g_shift1", "g_ob")):
            got[name] = mine(vec[8 + j])
    order = (
        "os", "ol", "dxs", "dxl", "gq", "g_qb", "gk", "gv", "g_vb", "gout", "g_ob", "g_gain1", "g_shift1",
        "gup", "g_ub", "gdown", "g_db", "g_gain2", "g_shift2",
    )
    return tuple(got[n].reshape(-1) if n.startswith("g_") else got[n] for n in order)


def solution(mesh):
    in_specs = (
        P("dp", None, None), P("dp", None, None), P(None, "mp"), P("mp"), P(None, "mp"), P(None, "mp"), P("mp"),
        P("mp", None), P(), P(), P(), P(None, "mp"), P("mp"), P("mp", None), P(), P(), P(),
        P("dp", None, None), P("dp", None, None), P("dp"), P("dp"), P("dp", None),
    )
    out_specs = (
        P("dp", None, None), P("dp", None, None), P("dp", None, None), P("dp", None, None),
        P("dp", "mp"), P(("mp", "dp")), P("dp", "mp"), P("dp", "mp"), P(("mp", "dp")), P("mp", "dp"),
        P("dp"), P("dp"), P("dp"), P("dp", "mp"), P(("mp", "dp")), P("mp", "dp"), P("dp"), P("dp"), P("dp"),
    )
    return jax.shard_map(
        functools.partial(shards, mesh.shape["dp"]),
        mesh=mesh, in_specs=in_specs, out_specs=out_specs, check_vma=False,
    )
```

```python
import functools

import jax
import jax.numpy as jnp
from jax import lax
from jax.experimental import pallas as pl
from jax.experimental.pallas import tpu as pltpu
from jax.sharding import PartitionSpec as P

HEAD = 64
PAIR = 2 * HEAD
NEGATIVE = -1e30
EPSILON = 1e-12
BF = jnp.bfloat16
F32 = jnp.float32
MESH = pl.DeviceIdType.MESH

BITS = 4
X, Y, NEAR, FAR = 0, 1, 2, 3
ORDERS = (
    (X, Y, NEAR, FAR),
    (Y, NEAR, X, FAR),
    (NEAR, X, Y, FAR),
    (X, NEAR, Y, FAR),
    (Y, X, NEAR, FAR),
    (NEAR, Y, X, FAR),
)
PARTS_AT = (0, 8, 12, 14)


def mm(left, right):
    return jnp.dot(left, right, preferred_element_type=F32)


def mm_nt(left, right):
    return lax.dot_general(left, right, (((1,), (1,)), ((), ())), preferred_element_type=F32)


def mm_tn(left, right):
    return lax.dot_general(left, right, (((0,), (0,)), ((), ())), preferred_element_type=F32)


def rows_of(start, size):
    return pl.ds(pl.multiple_of(start, size), size)


def fold(values):
    rows, width = values.shape
    return jnp.sum(values.reshape(rows // 8, 8, width), axis=0)


def place(order, block):
    spot = 0
    for bit in order:
        spot = spot * 2 + ((block >> bit) & 1)
    return spot


class Refs:
    pass


def layer(reduce_here, names, *refs):
    r = Refs()
    for name, ref in zip(names, refs, strict=True):
        setattr(r, name, ref)
    dp, mp = lax.axis_index("dp"), lax.axis_index("mp")
    peer = (dp, 1 - mp)
    half = r.own.shape[1]
    seg_rows = 2 * half
    width = r.x.shape[1]
    local = r.q.shape[1]
    pairs = local // PAIR
    heads = local // HEAD
    hidden = r.f.shape[1]
    short_slots, short_length = r.xs.shape[0], r.xs.shape[1]
    long_length = r.xl.shape[1]
    block = r.G0.shape[1]
    tile = 64

    my_bit = [lax.rem(lax.div(dp, 1 << k), 2) for k in range(BITS)]
    across = [(dp + (1 - 2 * my_bit[k]) * (1 << k), mp) for k in range(BITS)]

    loads = {}

    def load(name, src, dst):
        cp = pltpu.make_async_copy(src, dst, r.load_sem.at[len(loads)])
        cp.start()
        loads[name] = cp

    load("xl", r.xl.at[0], r.x.at[pl.ds(seg_rows, seg_rows)])
    load("wq", r.wq_h, r.wq)
    load("wk", r.wk_h, r.wk)
    load("wv", r.wv_h, r.wv)
    for s in range(short_slots):
        load(f"xs{s}", r.xs.at[s], r.x.at[pl.ds(s * short_length, short_length)])
    load("wo", r.wo_h, r.wo)
    load("wu", r.wu_h, r.wu)
    load("wd", r.wd_h, r.wd)
    load("us", r.us.at[pl.ds(mp * (short_slots // 2), short_slots // 2)], r.ups)
    load("ul", r.ul.at[0, rows_of(mp * half, half)], r.upl)

    barrier = pltpu.get_barrier_semaphore()
    partners = [peer] + (across if reduce_here else [])
    for other in partners:
        pl.semaphore_signal(barrier, inc=1, device_id=other, device_id_type=MESH)

    sends = []

    def remote(src, dst, index, device):
        cp = pltpu.make_async_remote_copy(
            src_ref=src,
            dst_ref=dst,
            send_sem=r.ex_send.at[index],
            recv_sem=r.ex_recv.at[index],
            device_id=device,
            device_id_type=MESH,
        )
        cp.start()
        sends.append(cp)
        return cp

    live_short, live_long = r.live[0, 0], r.live[0, 1]
    long_len = jnp.where(live_long > 0, r.ll[0], 0)

    def short_len(slot):
        return jnp.where(slot < live_short, r.sl[slot], 0)

    def param(ref):
        return ref[...].astype(F32).reshape(1, -1)

    qb, vb, ob, g1, b1 = (param(n) for n in (r.qb, r.vb, r.ob, r.g1, r.b1))
    ub, db, g2, b2 = (param(n) for n in (r.ub, r.db, r.g2, r.b2))

    low_lane = lax.broadcasted_iota(jnp.int32, (1, PAIR), 1) < HEAD

    def first(values):
        return jnp.where(low_lane, values, jnp.zeros_like(values))

    def second(values):
        return jnp.where(low_lane, jnp.zeros_like(values), values)

    def own_start(seg):
        return seg * seg_rows + mp * half

    def peer_start(seg):
        return seg * seg_rows + (1 - mp) * half

    r.acc[...] = jnp.zeros_like(r.acc)
    r.acc_up[...] = jnp.zeros_like(r.acc_up)
    r.acc_qv[...] = jnp.zeros_like(r.acc_qv)

    def project(seg):
        rows = slice(seg * seg_rows, (seg + 1) * seg_rows)
        tokens = r.x[rows, :]
        r.q[rows, :] = (mm(tokens, r.wq[...]) + qb).astype(BF) * BF(HEAD**-0.5)
        r.k[rows, :] = mm(tokens, r.wk[...]).astype(BF)
        r.v[rows, :] = (mm(tokens, r.wv[...]) + vb).astype(BF)

    def softmax(scores):
        highest = [jnp.max(s, axis=-1, keepdims=True) for s in scores]
        expo = [jnp.exp(s - m) for s, m in zip(scores, highest)]
        total = [1.0 / jnp.sum(e, axis=-1, keepdims=True) for e in expo]
        return [(e * t).astype(BF) for e, t in zip(expo, total)]

    def lanes_of(pair):
        return slice(pair * PAIR, (pair + 1) * PAIR)

    def slot_rows(s):
        return slice(s * short_length, (s + 1) * short_length)

    long_rows = slice(seg_rows, 2 * seg_rows)

    def attend_long():
        position = lax.broadcasted_iota(jnp.int32, (1, long_length), 1)
        bias = jnp.where(position < long_len, 0.0, NEGATIVE)
        for pair in range(pairs):
            lanes = lanes_of(pair)
            qp, kp, vp = r.q[long_rows, lanes], r.k[long_rows, lanes], r.v[long_rows, lanes]
            parts = []
            for j, pick in enumerate((first, second)):
                (probs,) = softmax([mm_nt(pick(qp), kp) + bias])
                r.pl[2 * pair + j] = probs
                parts.append(mm(probs, vp))
            r.ctx[long_rows, lanes] = jnp.where(low_lane, *parts).astype(BF)

    def attend_short():
        position = lax.broadcasted_iota(jnp.int32, (1, short_length), 1)
        scores = []
        for s in range(short_slots):
            bias = jnp.where(position < short_len(s), 0.0, NEGATIVE)
            for pair in range(pairs):
                qp, kp = r.q[slot_rows(s), lanes_of(pair)], r.k[slot_rows(s), lanes_of(pair)]
                scores += [mm_nt(first(qp), kp) + bias, mm_nt(second(qp), kp) + bias]
        probs = softmax(scores)
        for s in range(short_slots):
            for pair in range(pairs):
                parts = []
                for head in (2 * pair, 2 * pair + 1):
                    r.ps[s, head] = probs[s * heads + head]
                    parts.append(mm(probs[s * heads + head], r.v[slot_rows(s), lanes_of(pair)]))
                r.ctx[slot_rows(s), lanes_of(pair)] = jnp.where(low_lane, *parts).astype(BF)

    def exchange(stage, seg, left, right, product, between=lambda: None):
        index = 2 * stage + seg
        r.out_buf[index] = product(left[rows_of(peer_start(seg), half), :], right[...]).astype(BF)
        cp = remote(r.out_buf.at[index], r.in_buf.at[index], index, peer)
        between()
        r.own[seg] = product(left[rows_of(own_start(seg), half), :], right[...])
        return cp

    def share(index, seg, ref):
        rows = rows_of(own_start(seg), half)
        return remote(ref.at[rows], ref.at[rows], index, peer)

    def norm(values):
        mean = jnp.mean(values, axis=-1, keepdims=True)
        centred = values - mean
        scale = lax.rsqrt(jnp.mean(centred * centred, axis=-1, keepdims=True) + EPSILON)
        return centred * scale, scale

    def norm_back(normed, scale, grad):
        return scale * (
            grad
            - jnp.mean(grad, axis=-1, keepdims=True)
            - normed * jnp.mean(grad * normed, axis=-1, keepdims=True)
        )

    def norm_one(seg):
        for t in range(half // tile):
            mine = slice(seg * half + t * tile, seg * half + (t + 1) * tile)
            here = slice(t * tile, (t + 1) * tile)
            rows = rows_of(own_start(seg) + t * tile, tile)
            total = r.own[seg, here, :] + r.in_buf[seg, here, :].astype(F32) + ob
            normed, scale = norm(r.x[rows, :].astype(F32) + total)
            r.n1[mine, :] = normed
            r.r1[mine, :] = scale
            r.h[rows, :] = (normed * g1 + b1).astype(BF)

    def up(start):
        rows = rows_of(start, half)
        step = 512
        for j in range(hidden // step):
            cols = slice(j * step, (j + 1) * step)
            pre = mm(r.h[rows, :], r.wu[:, cols]) + ub[:, cols]
            phi = 0.5 + 0.5 * lax.erf(pre * (0.5**0.5))
            r.f[rows, cols] = (pre * phi).astype(BF)
            r.gp[rows, cols] = (phi + pre * (jnp.exp(pre * pre * -0.5) * 0.3989422804014327)).astype(BF)

    def norm_two(seg):
        for t in range(half // tile):
            mine = slice(seg * half + t * tile, seg * half + (t + 1) * tile)
            here = slice(t * tile, (t + 1) * tile)
            rows = rows_of(own_start(seg) + t * tile, tile)
            row = lax.broadcasted_iota(jnp.int32, (tile, 1), 0)
            if seg == 0:
                slot, inner = t * tile // short_length, t * tile % short_length
                keep = row + inner < short_len(mp * (short_slots // 2) + slot)
                upstream = r.ups[slot, inner : inner + tile, :]
            else:
                keep = row + (mp * half + t * tile) < long_len
                upstream = r.upl[here, :]
            keep = keep.astype(F32)
            hidden_state = r.n1[mine, :] * g1 + b1
            total = r.own[seg, here, :] + r.in_buf[2 + seg, here, :].astype(F32) + db
            normed, scale = norm(hidden_state + total)
            r.out[seg, here, :] = (keep * (normed * g2 + b2)).astype(BF)
            grad = keep * upstream.astype(F32)
            r.acc[0] += fold(grad * normed)
            r.acc[1] += fold(grad)
            dsecond = norm_back(normed, scale, grad * g2)
            low = dsecond.astype(BF)
            r.acc[2] += fold(low.astype(F32))
            r.ds[mine, :] = dsecond
            r.do[rows, :] = low

    def norm_one_back(seg):
        for t in range(half // tile):
            mine = slice(seg * half + t * tile, seg * half + (t + 1) * tile)
            here = slice(t * tile, (t + 1) * tile)
            rows = rows_of(own_start(seg) + t * tile, tile)
            grad = r.ds[mine, :] + r.own[seg, here, :] + r.in_buf[4 + seg, here, :].astype(F32)
            normed = r.n1[mine, :]
            r.acc[3] += fold(grad * normed)
            r.acc[4] += fold(grad)
            dfirst = norm_back(normed, r.r1[mine, :], grad * g1)
            low = dfirst.astype(BF)
            r.acc[5] += fold(low.astype(F32))
            r.ds[mine, :] = dfirst
            r.da[rows, :] = low

    def active_back(seg):
        for part in range(2):
            rows = slice(seg * seg_rows + part * half, seg * seg_rows + (part + 1) * half)
            step = 512
            for j in range(hidden // step):
                yield
                cols = slice(j * step, (j + 1) * step)
                low = (mm_nt(r.do[rows, :], r.wd[cols, :]) * r.gp[rows, cols].astype(F32)).astype(BF)
                r.acc_up[:, cols] += fold(low.astype(F32))
                r.gp[rows, cols] = low

    def dscores(rows, lanes, probs):
        vp, dc = r.v[rows, lanes], r.dctx[rows, lanes]
        product = dc.astype(F32) * r.ctx[rows, lanes].astype(F32)
        held = []
        for j, pick in enumerate((first, second)):
            inner = jnp.sum(pick(product), axis=-1, keepdims=True)
            held.append((probs[j].astype(F32) * (mm_nt(pick(dc), vp) - inner)).astype(BF))
        return held

    def heads_back(rows, lanes, probs, held):
        qp, kp, dc = r.q[rows, lanes], r.k[rows, lanes], r.dctx[rows, lanes]
        r.dq[rows, lanes] = (jnp.where(low_lane, mm(held[0], kp), mm(held[1], kp)) * HEAD**-0.5).astype(BF)
        r.dk[rows, lanes] = jnp.where(low_lane, mm_tn(held[0], qp), mm_tn(held[1], qp)).astype(BF)
        r.dv[rows, lanes] = jnp.where(low_lane, mm_tn(probs[0], dc), mm_tn(probs[1], dc)).astype(BF)

    def attend_long_back(pair):
        probs = [r.pl[2 * pair], r.pl[2 * pair + 1]]
        held = dscores(long_rows, lanes_of(pair), probs)
        r.dS[0], r.dS[1] = held
        heads_back(long_rows, lanes_of(pair), probs, [r.dS[0], r.dS[1]])

    def attend_short_back():
        each = [(s, pair) for s in range(short_slots) for pair in range(pairs)]
        probs = [[r.ps[s, 2 * pair], r.ps[s, 2 * pair + 1]] for s, pair in each]
        held = [dscores(slot_rows(s), lanes_of(pair), p) for (s, pair), p in zip(each, probs)]
        for (s, pair), p, h in zip(each, probs, held):
            heads_back(slot_rows(s), lanes_of(pair), p, h)

    begin, flight = {}, {}

    def half_copy(c, p):
        n = 8 >> p
        bit = ORDERS[KINDS[c]][p]
        start = begin.get(c, 0)
        held, landed = getattr(r, f"G{c}"), getattr(r, f"R{c}")
        cp = pltpu.make_async_remote_copy(
            src_ref=held.at[pl.ds(start + (1 - my_bit[bit]) * n, n)],
            dst_ref=landed.at[pl.ds(PARTS_AT[p], n)],
            send_sem=r.rs_send.at[c, p],
            recv_sem=r.rs_recv.at[c, p],
            device_id=across[bit],
            device_id_type=MESH,
        )
        cp.start()
        sends.append(cp)
        begin[c] = start + my_bit[bit] * n
        flight[c] = (p, cp)

    def operands(start, stop):
        for left, right in ((r.do, r.f), (r.h, r.gp), (r.da, r.ctx), (r.x, r.dq), (r.x, r.dk), (r.x, r.dv)):
            span = right.shape[1]
            if start < span:
                return left, right[:, start:stop]
            start, stop = start - span, stop - span

    def gradient(c):
        order = ORDERS[KINDS[c]] if reduce_here else (3, 2, 1, 0)
        held = getattr(r, f"G{c}")
        blocks = 1 << BITS
        left, right = operands(COLUMNS[c], COLUMNS[c + 1])
        for m in range(2):
            part = width // 2
            piece = mm_tn(left[:, m * part : (m + 1) * part], right).astype(BF)
            for b in range(blocks // 2):
                held[place(order, m * blocks // 2 + b)] = piece[b * block : (b + 1) * block]
        if reduce_here:
            half_copy(c, 0)

    def advance(c):
        p, cp = flight.pop(c)
        n = 8 >> p
        held, landed = getattr(r, f"G{c}"), getattr(r, f"R{c}")
        cp.wait_recv()
        if p < BITS - 1:
            mine = pl.ds(begin[c], n)
            held[mine] = held[mine] + landed[PARTS_AT[p] : PARTS_AT[p] + n]
            half_copy(c, p + 1)
        else:
            total = held[begin[c]].astype(F32) + landed[PARTS_AT[p]].astype(F32)
            r.rows[:, COLUMNS[c] : COLUMNS[c + 1]] = total

    todo = list(EVENTS) if reduce_here else []
    marks = list(MARKS)

    def point():
        upto = marks.pop(0) if marks else len(EVENTS)
        while todo and len(EVENTS) - len(todo) < upto:
            advance(todo.pop(0))

    def gradients(group):
        for c, kind in enumerate(GROUPS):
            if kind == group:
                point()
                gradient(c)

    for name in ("xl", "wq", "wk", "wv"):
        loads[name].wait()
    project(1)
    attend_long()
    for s in range(short_slots):
        loads[f"xs{s}"].wait()
    loads["wo"].wait()
    pl.semaphore_wait(barrier, len(partners))
    ex = {}
    ex["a1"] = exchange(0, 1, r.ctx, r.wo, mm)
    project(0)
    attend_short()
    ex["a0"] = exchange(0, 0, r.ctx, r.wo, mm)
    loads["wu"].wait()
    loads["wd"].wait()
    ex["a1"].wait_recv()
    norm_one(1)
    ex["h1"] = share(8, 1, r.h)
    ex["a0"].wait_recv()
    norm_one(0)
    ex["h0"] = share(9, 0, r.h)
    for seg in (1, 0):
        up(own_start(seg))
        ex[f"h{seg}"].wait_recv()
        up(peer_start(seg))
        ex[f"o{seg}"] = exchange(1, seg, r.f, r.wd, mm)
    loads["us"].wait()
    loads["ul"].wait()
    outs, arrivals = [], []

    def publish(index, seg, short_ref, long_ref, held):
        if seg == 0:
            for s in range(short_slots // 2):
                piece = held.at[0, pl.ds(s * short_length, short_length)]
                target = short_ref.at[mp * (short_slots // 2) + s]
                cp = pltpu.make_async_copy(piece, target, r.out_sem.at[index + s])
                cp.start()
                outs.append(cp)
                arrivals.append(remote(piece, target, 16 + index + s, peer))
        else:
            target = long_ref.at[0, rows_of(mp * half, half)]
            cp = pltpu.make_async_copy(held.at[1], target, r.out_sem.at[index + 2])
            cp.start()
            outs.append(cp)
            arrivals.append(remote(held.at[1], target, 16 + index + 2, peer))

    for seg in (1, 0):
        ex[f"o{seg}"].wait_recv()
        norm_two(seg)
        ex[f"do{seg}"] = share(10 + seg, seg, r.do)
    ex["do1"].wait_recv()

    early, late = active_back(1), active_back(0)
    for _ in range(EARLY):
        next(early)
    ex["do0"].wait_recv()
    gradients("d")
    point()
    publish(0, 1, r.os, r.ol, r.out)
    publish(0, 0, r.os, r.ol, r.out)
    for pieces in (early, late):
        for _ in pieces:
            point()
    gradients("u")
    for seg in (1, 0):
        point()
        ex[f"dh{seg}"] = exchange(2, seg, r.gp, r.wu, mm_nt, point)
    for seg in (1, 0):
        point()
        ex[f"dh{seg}"].wait_recv()
        norm_one_back(seg)
        ex[f"da{seg}"] = share(12 + seg, seg, r.da)
    for seg in (1, 0):
        point()
        ex[f"da{seg}"].wait_recv()
        rows = slice(seg * seg_rows, (seg + 1) * seg_rows)
        r.dctx[rows, :] = mm_nt(r.da[rows, :], r.wo[...]).astype(BF)
    gradients("o")
    for pair in range(pairs):
        point()
        attend_long_back(pair)
    point()
    attend_short_back()
    gradients("q")
    point()
    r.acc_qv[:, :local] = fold(r.dq[...].astype(F32))
    r.acc_qv[:, local:] = fold(r.dv[...].astype(F32))

    def total_of(values):
        return jnp.sum(values, axis=0, keepdims=True)

    r.vec[...] = jnp.zeros_like(r.vec)
    r.vec[0:1, :] = total_of(r.acc_qv[...])
    r.vec[1:2, :] = total_of(r.acc_up[:, :width])
    r.vec[2:3, :] = total_of(r.acc_up[:, width:])
    for j in range(6):
        r.vec[8 + j : 9 + j, :] = total_of(r.acc[j])
    r.vec_out[0] = r.vec[...]
    vec_copy = remote(r.vec_out.at[0, pl.ds(8, 8)], r.vec_in.at[0, pl.ds(8, 8)], 14, peer)

    def input_part(rows):
        return (
            mm_nt(r.dq[rows, :], r.wq[...])
            + mm_nt(r.dk[rows, :], r.wk[...])
            + mm_nt(r.dv[rows, :], r.wv[...])
        )

    for seg in (1, 0):
        index = 6 + seg
        point()
        r.out_buf[index] = input_part(rows_of(peer_start(seg), half)).astype(BF)
        ex[f"dx{seg}"] = remote(r.out_buf.at[index], r.in_buf.at[index], index, peer)
        point()
        r.own[seg] = input_part(rows_of(own_start(seg), half))
    vec_copy.wait_recv()
    r.vec[8:16, :] = r.vec[8:16, :] + r.vec_in[0, 8:16, :]
    if reduce_here:
        r.vec_out[1] = r.vec[...]
        vec_copy = remote(r.vec_out.at[1], r.vec_in.at[1], 15, across[0])
    for seg in (1, 0):
        point()
        ex[f"dx{seg}"].wait_recv()
        dfirst = r.ds[seg * half : (seg + 1) * half, :]
        r.dxo[seg] = (dfirst + r.own[seg] + r.in_buf[6 + seg].astype(F32)).astype(BF)
        publish(3, seg, r.dxs, r.dxl, r.dxo)
    if reduce_here:
        left = len(todo)
        for k in range(1, BITS + 1):
            for _ in range(left // (BITS + 1)):
                advance(todo.pop(0))
            vec_copy.wait_recv()
            r.vec[...] = r.vec[...] + r.vec_in[k]
            if k < BITS:
                r.vec_out[k + 1] = r.vec[...]
                vec_copy = remote(r.vec_out.at[k + 1], r.vec_in.at[k + 1], 21 + k, across[k])
        while todo:
            advance(todo.pop(0))
    else:
        for c in range(len(GROUPS)):
            cp = pltpu.make_async_copy(
                getattr(r, f"G{c}"), r.grads.at[:, :, pl.ds(COLUMNS[c], COLUMNS[c + 1] - COLUMNS[c])], r.out_sem.at[6]
            )
            cp.start()
            cp.wait()
    r.sums[...] = r.vec[...]

    for cp in outs:
        cp.wait()
    for cp in arrivals:
        cp.wait_recv()
    for cp in sends:
        cp.wait_send()


COLUMNS = (
    0, 384, 768, 1152, 1536, 1920, 2304, 2688, 3072, 3456, 3840, 4224, 4608,
)
GROUPS = "dddduuuuoqqq"
KINDS = (
    2, 4, 3, 5, 0, 4, 4, 0, 2, 4, 5, 0,
)
EVENTS = (
    0, 1, 2, 3, 5, 4, 2, 6, 7, 8, 3, 0, 4, 1, 10, 2, 5, 4, 1, 6, 9, 2, 5, 4, 7, 1, 6, 11, 0, 5, 7, 10, 8, 6, 0,
    3, 11, 7, 8, 9, 3, 11, 10, 8, 9, 11, 10, 9,
)
MARKS = (
    0, 0, 0, 0, 0, 0, 0, 0, 0, 0, 0, 0, 0, 0, 0, 0, 0, 2, 3, 3, 3, 3, 3, 3, 3, 4, 5, 6, 7, 7, 7, 8, 9, 9, 10,
    10, 12, 12, 12, 13,
)
EARLY = 4


def shards(n_dp, *args):
    (
        xs, xl, wq, qb, wk, wv, vb, wo, ob, g1, b1, wu, ub, wd, db, g2, b2, us, ul, sl, ll, live,
    ) = args
    short_slots, short_length, width = xs.shape
    long_length = xl.shape[1]
    local, hidden = wq.shape[1], wu.shape[1]
    heads = local // HEAD
    rows = short_slots * short_length + xl.shape[0] * long_length
    half = long_length // 2
    reduce_here = n_dp == 1 << BITS
    blocks = 1 << BITS
    block = width // blocks
    columns = 4 * local + 2 * hidden
    spans = [COLUMNS[c + 1] - COLUMNS[c] for c in range(len(GROUPS))]
    assert COLUMNS[-1] == columns
    any_spec = pl.BlockSpec(memory_space=pl.ANY)
    vmem = pl.BlockSpec(memory_space=pltpu.VMEM)
    smem = pl.BlockSpec(memory_space=pltpu.SMEM)
    inputs = [
        ("sl", sl, smem), ("ll", ll, smem), ("live", live, smem),
        ("xs", xs, any_spec), ("xl", xl, any_spec), ("us", us, any_spec), ("ul", ul, any_spec),
        ("wq_h", wq, any_spec), ("wk_h", wk, any_spec), ("wv_h", wv, any_spec), ("wo_h", wo, any_spec),
        ("wu_h", wu, any_spec), ("wd_h", wd, any_spec),
        ("qb", qb, vmem), ("vb", vb, vmem), ("ob", ob, vmem), ("g1", g1, vmem), ("b1", b1, vmem),
        ("ub", ub, vmem), ("db", db, vmem), ("g2", g2, vmem), ("b2", b2, vmem),
    ]
    sds = jax.ShapeDtypeStruct
    outputs = [
        ("os", sds(xs.shape, BF), any_spec), ("ol", sds(xl.shape, BF), any_spec),
        ("dxs", sds(xs.shape, BF), any_spec), ("dxl", sds(xl.shape, BF), any_spec),
    ]
    if reduce_here:
        outputs.append(("rows", sds((block, columns), F32), vmem))
    else:
        outputs.append(("grads", sds((blocks, block, columns), BF), any_spec))
    outputs.append(("sums", sds((16, width), F32), vmem))
    v = pltpu.VMEM
    dma = pltpu.SemaphoreType.DMA
    scratch = [
        ("x", v((rows, width), BF)), ("ups", v((short_slots // 2, short_length, width), BF)), ("upl", v((half, width), BF)),
        ("wq", v(wq.shape, BF)), ("wk", v(wk.shape, BF)), ("wv", v(wv.shape, BF)), ("wo", v(wo.shape, BF)),
        ("wu", v(wu.shape, BF)), ("wd", v(wd.shape, BF)),
        ("q", v((rows, local), BF)), ("k", v((rows, local), BF)), ("v", v((rows, local), BF)),
        ("pl", v((heads, long_length, long_length), BF)), ("ps", v((short_slots, heads, short_length, short_length), BF)),
        ("ctx", v((rows, local), BF)), ("n1", v((2 * half, width), F32)), ("r1", v((2 * half, 1), F32)),
        ("h", v((rows, width), BF)), ("f", v((rows, hidden), BF)), ("gp", v((rows, hidden), BF)),
        ("do", v((rows, width), BF)), ("ds", v((2 * half, width), F32)), ("da", v((rows, width), BF)),
        ("dctx", v((rows, local), BF)), ("dq", v((rows, local), BF)), ("dk", v((rows, local), BF)), ("dv", v((rows, local), BF)),
        ("dS", v((2, long_length, long_length), BF)),
        ("own", v((2, half, width), F32)), ("out_buf", v((8, half, width), BF)), ("in_buf", v((8, half, width), BF)),
        ("out", v((2, half, width), BF)), ("dxo", v((2, half, width), BF)),
        ("acc", v((6, 8, width), F32)), ("acc_up", v((8, hidden), F32)), ("acc_qv", v((8, 2 * local), F32)),
        ("vec", v((16, width), F32)), ("vec_out", v((5, 16, width), F32)), ("vec_in", v((5, 16, width), F32)),
        ("load_sem", dma((16,))), ("out_sem", dma((8,))), ("ex_send", dma((28,))), ("ex_recv", dma((28,))),
        ("rs_send", dma((len(spans), BITS))), ("rs_recv", dma((len(spans), BITS))),
    ]
    for c, span in enumerate(spans):
        scratch.append((f"G{c}", v((blocks, block, span), BF)))
        scratch.append((f"R{c}", v((blocks - 1 if reduce_here else 1, block, span), BF)))
    names = [n for n, *_ in inputs] + [n for n, *_ in outputs] + [n for n, *_ in scratch]
    macs = rows * width * (8 * local + 6 * hidden)
    results = pl.pallas_call(
        functools.partial(layer, reduce_here, names),
        out_shape=[o[1] for o in outputs],
        in_specs=[i[2] for i in inputs],
        out_specs=[o[2] for o in outputs],
        scratch_shapes=[s[1] for s in scratch],
        cost_estimate=pl.CostEstimate(flops=2 * macs, bytes_accessed=20 << 20, transcendentals=0),
        compiler_params=pltpu.CompilerParams(
            collective_id=0, has_side_effects=True, vmem_limit_bytes=62 << 20
        ),
    )(*[i[1] for i in inputs])
    got = dict(zip([o[0] for o in outputs], results, strict=True))
    if not reduce_here:
        grads = got["grads"].reshape(width, columns).astype(F32)
        got["rows"] = lax.psum_scatter(grads, "dp", scatter_dimension=0, tiled=True)
        got["sums"] = lax.psum(got["sums"], "dp")
    block = width // n_dp
    finals = [
        ("os", sds(xs.shape, BF), any_spec), ("ol", sds(xl.shape, BF), any_spec),
        ("dxs", sds(xs.shape, BF), any_spec), ("dxl", sds(xl.shape, BF), any_spec),
        ("gq", sds((block, local), F32), vmem), ("g_qb", sds((local // n_dp,), F32), vmem),
        ("gk", sds((block, local), F32), vmem), ("gv", sds((block, local), F32), vmem),
        ("g_vb", sds((local // n_dp,), F32), vmem), ("gout", sds((block, local), F32), vmem),
        ("g_ob", sds((block,), F32), vmem), ("g_gain1", sds((block,), F32), vmem), ("g_shift1", sds((block,), F32), vmem),
        ("gup", sds((block, hidden), F32), vmem), ("g_ub", sds((hidden // n_dp,), F32), vmem),
        ("gdown", sds((block, hidden), F32), vmem),
        ("g_db", sds((block,), F32), vmem), ("g_gain2", sds((block,), F32), vmem), ("g_shift2", sds((block,), F32), vmem),
    ]
    sources = ("os", "ol", "dxs", "dxl", "rows", "sums")
    names = ["in_" + n for n in sources] + [f[0] for f in finals] + ["held_" + n for n in sources[:4]] + ["sem"]
    results = pl.pallas_call(
        functools.partial(place_results, n_dp, names),
        out_shape=[f[1] for f in finals],
        in_specs=[any_spec] * 4 + [vmem] * 2,
        out_specs=[f[2] for f in finals],
        scratch_shapes=[v(f[1].shape, BF) for f in finals[:4]] + [dma((8,))],
        cost_estimate=pl.CostEstimate(flops=0, bytes_accessed=8 << 20, transcendentals=0),
        compiler_params=pltpu.CompilerParams(vmem_limit_bytes=62 << 20),
    )(*[got[n] for n in sources])
    return tuple(result.T if f[0] in ("gout", "gdown") else result for f, result in zip(finals, results, strict=True))


def place_results(n_dp, names, *refs):
    r = Refs()
    for name, ref in zip(names, refs, strict=True):
        setattr(r, name, ref)
    big = ("os", "ol", "dxs", "dxl")
    into = [pltpu.make_async_copy(getattr(r, "in_" + n), getattr(r, "held_" + n), r.sem.at[j]) for j, n in enumerate(big)]
    out = [pltpu.make_async_copy(getattr(r, "held_" + n), getattr(r, n), r.sem.at[4 + j]) for j, n in enumerate(big)]
    for cp in into:
        cp.start()
    for cp, back in zip(into, out):
        cp.wait()
        back.start()
    dp = lax.axis_index("dp")
    hidden, local = r.gup.shape[1], r.gq.shape[1]
    width = r.in_sums.shape[1]
    r.gdown[...] = r.in_rows[:, :hidden]
    r.gup[...] = r.in_rows[:, hidden : 2 * hidden]
    at = 2 * hidden
    r.gout[...] = r.in_rows[:, at : at + local]
    for j, ref in enumerate((r.gq, r.gk, r.gv)):
        ref[...] = r.in_rows[:, at + (j + 1) * local : at + (j + 2) * local]

    def pick(row, size, start):
        turned = pltpu.roll(r.in_sums[...], lax.rem(2 * width - start, width), 1)
        return turned[row : row + 1, :size].reshape(size)

    size = r.g_ob.shape[0]
    for j, ref in enumerate((r.g_gain2, r.g_shift2, r.g_db, r.g_gain1, r.g_shift1, r.g_ob)):
        ref[...] = pick(8 + j, size, dp * size)
    size = r.g_qb.shape[0]
    r.g_qb[...] = pick(0, size, dp * size)
    r.g_vb[...] = pick(0, size, local + dp * size)
    size = r.g_ub.shape[0]
    lower = pick(1, size, lax.rem(dp * size, width))
    upper = pick(2, size, lax.rem(dp * size, width))
    r.g_ub[...] = jnp.where(dp * size < width, lower, upper)
    for cp in out:
        cp.wait()


def solution(mesh):
    in_specs = (
        P("dp", None, None), P("dp", None, None), P(None, "mp"), P("mp"), P(None, "mp"), P(None, "mp"), P("mp"),
        P("mp", None), P(), P(), P(), P(None, "mp"), P("mp"), P("mp", None), P(), P(), P(),
        P("dp", None, None), P("dp", None, None), P("dp"), P("dp"), P("dp", None),
    )
    out_specs = (
        P("dp", None, None), P("dp", None, None), P("dp", None, None), P("dp", None, None),
        P("dp", "mp"), P(("mp", "dp")), P("dp", "mp"), P("dp", "mp"), P(("mp", "dp")), P("mp", "dp"),
        P("dp"), P("dp"), P("dp"), P("dp", "mp"), P(("mp", "dp")), P("mp", "dp"), P("dp"), P("dp"), P("dp"),
    )
    return jax.shard_map(
        functools.partial(shards, mesh.shape["dp"]),
        mesh=mesh, in_specs=in_specs, out_specs=out_specs, check_vma=False,
    )
```

```python
import functools

import jax
import jax.numpy as jnp
from jax import lax
from jax.experimental import pallas as pl
from jax.experimental.pallas import tpu as pltpu
from jax.sharding import PartitionSpec as P

HEAD = 64
PAIR = 2 * HEAD
NEGATIVE = -1e30
EPSILON = 1e-12
BF = jnp.bfloat16
F32 = jnp.float32
MESH = pl.DeviceIdType.MESH

BITS = 4
X, Y, NEAR, FAR = 0, 1, 2, 3
ORDERS = (
    (X, Y, NEAR, FAR),
    (X, Y, FAR, NEAR),
    (X, NEAR, Y, FAR),
    (X, NEAR, FAR, Y),
    (X, FAR, Y, NEAR),
    (X, FAR, NEAR, Y),
    (Y, X, NEAR, FAR),
    (Y, X, FAR, NEAR),
    (Y, NEAR, X, FAR),
    (Y, NEAR, FAR, X),
    (Y, FAR, X, NEAR),
    (Y, FAR, NEAR, X),
    (NEAR, X, Y, FAR),
    (NEAR, X, FAR, Y),
    (NEAR, Y, X, FAR),
    (NEAR, Y, FAR, X),
    (NEAR, FAR, X, Y),
    (NEAR, FAR, Y, X),
)
PARTS_AT = (0, 8, 12, 14)


def mm(left, right):
    return jnp.dot(left, right, preferred_element_type=F32)


def mm_nt(left, right):
    return lax.dot_general(left, right, (((1,), (1,)), ((), ())), preferred_element_type=F32)


def mm_tn(left, right):
    return lax.dot_general(left, right, (((0,), (0,)), ((), ())), preferred_element_type=F32)


def rows_of(start, size):
    return pl.ds(pl.multiple_of(start, size), size)


def fold(values):
    rows, width = values.shape
    return jnp.sum(values.reshape(rows // 8, 8, width), axis=0)


def place(order, block):
    spot = 0
    for bit in order:
        spot = spot * 2 + ((block >> bit) & 1)
    return spot


class Refs:
    pass


def layer(reduce_here, names, *refs):
    r = Refs()
    for name, ref in zip(names, refs, strict=True):
        setattr(r, name, ref)
    dp, mp = lax.axis_index("dp"), lax.axis_index("mp")
    peer = (dp, 1 - mp)
    half = r.own.shape[1]
    seg_rows = 2 * half
    width = r.x.shape[1]
    local = r.ctx.shape[1]
    pairs = local // PAIR
    heads = local // HEAD
    hidden = r.f.shape[1]
    short_slots, short_length = r.xs.shape[0], r.xs.shape[1]
    long_length = r.xl.shape[1]
    block = r.G0.shape[1]
    tile = 64

    my_bit = [lax.rem(lax.div(dp, 1 << k), 2) for k in range(BITS)]
    across = [(dp + (1 - 2 * my_bit[k]) * (1 << k), mp) for k in range(BITS)]

    loads = {}

    def load(name, src, dst):
        cp = pltpu.make_async_copy(src, dst, r.load_sem.at[len(loads)])
        cp.start()
        loads[name] = cp

    load("xl", r.xl.at[0], r.x.at[pl.ds(seg_rows, seg_rows)])
    for j, source in enumerate((r.wq_h, r.wk_h, r.wv_h)):
        load(f"w{j}", source, r.wqkv.at[:, pl.ds(j * local, local)])

    def load_rest():
        for s in range(short_slots):
            load(f"xs{s}", r.xs.at[s], r.x.at[pl.ds(s * short_length, short_length)])
        load("wo", r.wo_h, r.wo)
        load("wu", r.wu_h, r.wu)
        load("wd", r.wd_h, r.wd)
        load("us", r.us.at[pl.ds(mp * (short_slots // 2), short_slots // 2)], r.ups)
        load("ul", r.ul.at[0, rows_of(mp * half, half)], r.upl)

    barrier = pltpu.get_barrier_semaphore()
    partners = [peer] + (across if reduce_here else [])
    for other in partners:
        pl.semaphore_signal(barrier, inc=1, device_id=other, device_id_type=MESH)

    sends = []

    def remote(src, dst, index, device):
        cp = pltpu.make_async_remote_copy(
            src_ref=src,
            dst_ref=dst,
            send_sem=r.ex_send.at[index],
            recv_sem=r.ex_recv.at[index],
            device_id=device,
            device_id_type=MESH,
        )
        cp.start()
        sends.append(cp)
        return cp

    live_short, live_long = r.live[0, 0], r.live[0, 1]
    long_len = jnp.where(live_long > 0, r.ll[0], 0)

    def short_len(slot):
        return jnp.where(slot < live_short, r.sl[slot], 0)

    def param(ref):
        return ref[...].astype(F32).reshape(1, -1)

    qb, vb, ob, g1, b1 = (param(n) for n in (r.qb, r.vb, r.ob, r.g1, r.b1))
    ub, db, g2, b2 = (param(n) for n in (r.ub, r.db, r.g2, r.b2))

    low_lane = lax.broadcasted_iota(jnp.int32, (1, PAIR), 1) < HEAD

    def first(values):
        return jnp.where(low_lane, values, jnp.zeros_like(values))

    def second(values):
        return jnp.where(low_lane, jnp.zeros_like(values), values)

    def own_start(seg):
        return seg * seg_rows + mp * half

    def peer_start(seg):
        return seg * seg_rows + (1 - mp) * half

    r.acc[...] = jnp.zeros_like(r.acc)
    r.acc_up[...] = jnp.zeros_like(r.acc_up)
    r.acc_qv[...] = jnp.zeros_like(r.acc_qv)

    def project(seg):
        rows = slice(seg * seg_rows, (seg + 1) * seg_rows)
        product = mm(r.x[rows, :], r.wqkv[...])
        r.qkv[rows, :local] = (product[:, :local] + qb).astype(BF) * BF(HEAD**-0.5)
        r.qkv[rows, local : 2 * local] = product[:, local : 2 * local].astype(BF)
        r.qkv[rows, 2 * local :] = (product[:, 2 * local :] + vb).astype(BF)

    def softmax(scores):
        highest = [jnp.max(s, axis=-1, keepdims=True) for s in scores]
        expo = [jnp.exp(s - m) for s, m in zip(scores, highest)]
        total = [1.0 / jnp.sum(e, axis=-1, keepdims=True) for e in expo]
        return [(e * t).astype(BF) for e, t in zip(expo, total)]

    def lanes_of(pair, part=0):
        if isinstance(pair, int):
            return slice(part * local + pair * PAIR, part * local + (pair + 1) * PAIR)
        return rows_of(part * local + pair * PAIR, PAIR)

    def parts_of(ref, rows, pair):
        return [ref[rows, lanes_of(pair, part)] for part in range(3)]

    def slot_rows(s):
        return slice(s * short_length, (s + 1) * short_length)

    long_rows = slice(seg_rows, 2 * seg_rows)

    def attend_long():
        position = lax.broadcasted_iota(jnp.int32, (1, long_length), 1)
        bias = jnp.where(position < long_len, 0.0, NEGATIVE)
        for pair in range(pairs):
            qp, kp, vp = parts_of(r.qkv, long_rows, pair)
            parts = []
            for j, pick in enumerate((first, second)):
                (probs,) = softmax([mm_nt(pick(qp), kp) + bias])
                r.pl[2 * pair + j] = probs
                parts.append(mm(probs, vp))
            r.ctx[long_rows, lanes_of(pair)] = jnp.where(low_lane, *parts).astype(BF)

    def attend_short():
        position = lax.broadcasted_iota(jnp.int32, (1, short_length), 1)
        scores = []
        for s in range(short_slots):
            bias = jnp.where(position < short_len(s), 0.0, NEGATIVE)
            for pair in range(pairs):
                qp, kp, _ = parts_of(r.qkv, slot_rows(s), pair)
                scores += [mm_nt(first(qp), kp) + bias, mm_nt(second(qp), kp) + bias]
        probs = softmax(scores)
        for s in range(short_slots):
            for pair in range(pairs):
                parts = []
                for head in (2 * pair, 2 * pair + 1):
                    r.ps[s, head] = probs[s * heads + head]
                    parts.append(mm(probs[s * heads + head], r.qkv[slot_rows(s), lanes_of(pair, 2)]))
                r.ctx[slot_rows(s), lanes_of(pair)] = jnp.where(low_lane, *parts).astype(BF)

    def exchange(stage, seg, left, right, product, between=lambda: None):
        index = 2 * stage + seg
        r.out_buf[index] = product(left[rows_of(peer_start(seg), half), :], right[...]).astype(BF)
        cp = remote(r.out_buf.at[index], r.in_buf.at[index], index, peer)
        between()
        r.own[seg] = product(left[rows_of(own_start(seg), half), :], right[...])
        return cp

    def share(index, seg, ref):
        rows = rows_of(own_start(seg), half)
        return remote(ref.at[rows], ref.at[rows], index, peer)

    def norm(values):
        mean = jnp.mean(values, axis=-1, keepdims=True)
        centred = values - mean
        scale = lax.rsqrt(jnp.mean(centred * centred, axis=-1, keepdims=True) + EPSILON)
        return centred * scale, scale

    def norm_back(normed, scale, grad):
        return scale * (
            grad
            - jnp.mean(grad, axis=-1, keepdims=True)
            - normed * jnp.mean(grad * normed, axis=-1, keepdims=True)
        )

    def norm_one(seg):
        for t in range(half // tile):
            mine = slice(seg * half + t * tile, seg * half + (t + 1) * tile)
            here = slice(t * tile, (t + 1) * tile)
            rows = rows_of(own_start(seg) + t * tile, tile)
            total = r.own[seg, here, :] + r.in_buf[seg, here, :].astype(F32) + ob
            normed, scale = norm(r.x[rows, :].astype(F32) + total)
            r.n1[mine, :] = normed
            r.r1[mine, :] = scale
            r.h[rows, :] = (normed * g1 + b1).astype(BF)

    def up(seg):
        rows = slice(seg * seg_rows, (seg + 1) * seg_rows)
        step = 256
        for j in range(hidden // step):
            cols = slice(j * step, (j + 1) * step)
            pre = mm(r.h[rows, :], r.wu[:, cols]) + ub[:, cols]
            phi = 0.5 + 0.5 * lax.erf(pre * (0.5**0.5))
            r.f[rows, cols] = (pre * phi).astype(BF)
            r.gp[rows, cols] = (phi + pre * (jnp.exp(pre * pre * -0.5) * 0.3989422804014327)).astype(BF)

    def norm_two(seg):
        for t in range(half // tile):
            mine = slice(seg * half + t * tile, seg * half + (t + 1) * tile)
            here = slice(t * tile, (t + 1) * tile)
            rows = rows_of(own_start(seg) + t * tile, tile)
            row = lax.broadcasted_iota(jnp.int32, (tile, 1), 0)
            if seg == 0:
                slot, inner = t * tile // short_length, t * tile % short_length
                keep = row + inner < short_len(mp * (short_slots // 2) + slot)
                upstream = r.ups[slot, inner : inner + tile, :]
            else:
                keep = row + (mp * half + t * tile) < long_len
                upstream = r.upl[here, :]
            keep = keep.astype(F32)
            hidden_state = r.n1[mine, :] * g1 + b1
            total = r.own[seg, here, :] + r.in_buf[2 + seg, here, :].astype(F32) + db
            normed, scale = norm(hidden_state + total)
            r.out[seg, here, :] = (keep * (normed * g2 + b2)).astype(BF)
            grad = keep * upstream.astype(F32)
            r.acc[0] += fold(grad * normed)
            r.acc[1] += fold(grad)
            dsecond = norm_back(normed, scale, grad * g2)
            low = dsecond.astype(BF)
            r.acc[2] += fold(low.astype(F32))
            r.ds[mine, :] = dsecond
            r.do[rows, :] = low

    def norm_one_back(seg):
        for t in range(half // tile):
            mine = slice(seg * half + t * tile, seg * half + (t + 1) * tile)
            here = slice(t * tile, (t + 1) * tile)
            rows = rows_of(own_start(seg) + t * tile, tile)
            grad = r.ds[mine, :] + r.own[seg, here, :] + r.in_buf[4 + seg, here, :].astype(F32)
            normed = r.n1[mine, :]
            r.acc[3] += fold(grad * normed)
            r.acc[4] += fold(grad)
            dfirst = norm_back(normed, r.r1[mine, :], grad * g1)
            low = dfirst.astype(BF)
            r.acc[5] += fold(low.astype(F32))
            r.ds[mine, :] = dfirst
            r.da[rows, :] = low

    def active_back(seg):
        for part in range(2):
            rows = slice(seg * seg_rows + part * half, seg * seg_rows + (part + 1) * half)
            step = 512
            for j in range(hidden // step):
                yield
                cols = slice(j * step, (j + 1) * step)
                low = (mm_nt(r.do[rows, :], r.wd[cols, :]) * r.gp[rows, cols].astype(F32)).astype(BF)
                r.acc_up[:, cols] += fold(low.astype(F32))
                r.gp[rows, cols] = low

    def dscores(rows, pair, probs):
        vp, dc = r.qkv[rows, lanes_of(pair, 2)], r.dctx[rows, lanes_of(pair)]
        product = dc.astype(F32) * r.ctx[rows, lanes_of(pair)].astype(F32)
        held = []
        for j, pick in enumerate((first, second)):
            inner = jnp.sum(pick(product), axis=-1, keepdims=True)
            held.append((probs[j].astype(F32) * (mm_nt(pick(dc), vp) - inner)).astype(BF))
        return held

    def heads_back(rows, pair, probs, held):
        qp, kp, _ = parts_of(r.qkv, rows, pair)
        dc = r.dctx[rows, lanes_of(pair)]
        dq = jnp.where(low_lane, mm(held[0], kp), mm(held[1], kp)) * HEAD**-0.5
        r.dqkv[rows, lanes_of(pair)] = dq.astype(BF)
        r.dqkv[rows, lanes_of(pair, 1)] = jnp.where(low_lane, mm_tn(held[0], qp), mm_tn(held[1], qp)).astype(BF)
        r.dqkv[rows, lanes_of(pair, 2)] = jnp.where(low_lane, mm_tn(probs[0], dc), mm_tn(probs[1], dc)).astype(BF)

    def attend_long_back(pair):
        probs = [r.pl[2 * pair], r.pl[2 * pair + 1]]
        heads_back(long_rows, pair, probs, dscores(long_rows, pair, probs))

    def attend_short_back():
        each = [(s, pair) for s in range(short_slots) for pair in range(pairs)]
        probs = [[r.ps[s, 2 * pair], r.ps[s, 2 * pair + 1]] for s, pair in each]
        held = [dscores(slot_rows(s), pair, p) for (s, pair), p in zip(each, probs)]
        for (s, pair), p, h in zip(each, probs, held):
            heads_back(slot_rows(s), pair, p, h)

    begin, flight = {}, {}

    def half_copy(c, p):
        n = 8 >> p
        bit = ORDERS[KINDS[c]][p]
        start = begin.get(c, 0)
        held, landed = getattr(r, f"G{c}"), getattr(r, f"R{c}")
        cp = pltpu.make_async_remote_copy(
            src_ref=held.at[pl.ds(start + (1 - my_bit[bit]) * n, n)],
            dst_ref=landed.at[pl.ds(PARTS_AT[p], n)],
            send_sem=r.rs_send.at[c, p],
            recv_sem=r.rs_recv.at[c, p],
            device_id=across[bit],
            device_id_type=MESH,
        )
        cp.start()
        sends.append(cp)
        begin[c] = start + my_bit[bit] * n
        flight[c] = (p, cp)

    def operands(start, stop):
        for left, right in ((r.do, r.f), (r.h, r.gp), (r.da, r.ctx), (r.x, r.dqkv)):
            span = right.shape[1]
            if start < span:
                return left, right, slice(start, stop)
            start, stop = start - span, stop - span

    def gradient(begins, ends):
        blocks = 1 << BITS
        part = width // 2
        base = COLUMNS[begins]
        left, right, cols = operands(base, COLUMNS[ends])
        orders = [ORDERS[KINDS[c]] if reduce_here else (3, 2, 1, 0) for c in range(begins, ends)]

        @pl.loop(0, 2)
        def _(m):
            piece = mm_tn(left[:, rows_of(m * part, part)], right[:, cols]).astype(BF)
            for c, order in zip(range(begins, ends), orders):
                held = getattr(r, f"G{c}")
                own = piece[:, COLUMNS[c] - base : COLUMNS[c + 1] - base]
                for b in range(blocks // 2):
                    held[place(order, b) + m * place(order, blocks // 2)] = own[b * block : (b + 1) * block]

        if reduce_here:
            for c in range(begins, ends):
                half_copy(c, 0)

    vector = [None, 0]

    def vector_copy(k):
        r.vec_out[k] = r.vec[...].astype(BF)
        device = peer if k == 0 else across[k - 1]
        vector[:] = remote(r.vec_out.at[k], r.vec_in.at[k], 22 + k, device), k

    def vector_advance():
        cp, k = vector
        cp.wait_recv()
        rows = slice(8 if k == 0 else 0, 16)
        r.vec[rows, :] = (r.vec_out[k].astype(F32) + r.vec_in[k].astype(F32))[rows]
        if k < BITS and reduce_here:
            vector_copy(k + 1)

    def advance(c):
        p, cp = flight.pop(c)
        n = 8 >> p
        held, landed = getattr(r, f"G{c}"), getattr(r, f"R{c}")
        cp.wait_recv()
        if p < BITS - 1:
            mine = pl.ds(begin[c], n)
            held[mine] = held[mine] + landed[PARTS_AT[p] : PARTS_AT[p] + n]
            half_copy(c, p + 1)
        else:
            total = held[begin[c]].astype(F32) + landed[PARTS_AT[p]].astype(F32)
            cols = slice(COLUMNS[c], COLUMNS[c + 1])
            r.held_rows[:, cols] = total
            cp = pltpu.make_async_copy(r.held_rows.at[:, cols], r.rows.at[:, cols], r.row_sem.at[c])
            cp.start()
            outs.append(cp)

    todo = list(EVENTS) if reduce_here else []
    marks = list(MARKS)

    def handle():
        c = todo.pop(0)
        if c < CHUNKS:
            advance(c)
        else:
            vector_advance()

    def point():
        upto = marks.pop(0) if marks else len(EVENTS)
        while todo and len(EVENTS) - len(todo) < upto:
            handle()

    def gradients(group):
        for job, begins, ends in JOBS:
            if job == group:
                point()
                gradient(begins, ends)

    for name in ("xl", "w0", "w1", "w2"):
        loads[name].wait()
    load_rest()
    project(1)
    attend_long()
    loads["wo"].wait()
    pl.semaphore_wait(barrier, len(partners))
    ex = {}
    ex["a1"] = exchange(0, 1, r.ctx, r.wo, mm)
    for s in range(short_slots):
        loads[f"xs{s}"].wait()
    project(0)
    ex["a1"].wait_recv()
    norm_one(1)
    ex["h1"] = share(8, 1, r.h)
    attend_short()
    ex["a0"] = exchange(0, 0, r.ctx, r.wo, mm)
    loads["wu"].wait()
    loads["wd"].wait()
    ex["h1"].wait_recv()
    up(1)
    ex["a0"].wait_recv()
    norm_one(0)
    ex["h0"] = share(9, 0, r.h)
    ex["o1"] = exchange(1, 1, r.f, r.wd, mm)
    ex["h0"].wait_recv()
    up(0)
    ex["o0"] = exchange(1, 0, r.f, r.wd, mm)
    loads["us"].wait()
    loads["ul"].wait()
    outs, arrivals = [], []

    def publish(index, seg, short_ref, long_ref, held):
        if seg == 0:
            for s in range(short_slots // 2):
                piece = held.at[0, pl.ds(s * short_length, short_length)]
                target = short_ref.at[mp * (short_slots // 2) + s]
                cp = pltpu.make_async_copy(piece, target, r.out_sem.at[index + s])
                cp.start()
                outs.append(cp)
                arrivals.append(remote(piece, target, 16 + index + s, peer))
        else:
            target = long_ref.at[0, rows_of(mp * half, half)]
            cp = pltpu.make_async_copy(held.at[1], target, r.out_sem.at[index + 2])
            cp.start()
            outs.append(cp)
            arrivals.append(remote(held.at[1], target, 16 + index + 2, peer))

    for seg in (1, 0):
        ex[f"o{seg}"].wait_recv()
        norm_two(seg)
        ex[f"do{seg}"] = share(10 + seg, seg, r.do)
    ex["do1"].wait_recv()

    early, late = active_back(1), active_back(0)
    for _ in range(EARLY):
        next(early)
    ex["do0"].wait_recv()
    gradients("d")
    point()
    publish(0, 1, r.os, r.ol, r.out)
    publish(0, 0, r.os, r.ol, r.out)
    for pieces in (early, late):
        for _ in pieces:
            point()
    gradients("u")
    for seg in (1, 0):
        point()
        ex[f"dh{seg}"] = exchange(2, seg, r.gp, r.wu, mm_nt, point)
    for seg in (1, 0):
        point()
        ex[f"dh{seg}"].wait_recv()
        norm_one_back(seg)
        ex[f"da{seg}"] = share(12 + seg, seg, r.da)
    for seg in (1, 0):
        point()
        ex[f"da{seg}"].wait_recv()
        rows = slice(seg * seg_rows, (seg + 1) * seg_rows)
        r.dctx[rows, :] = mm_nt(r.da[rows, :], r.wo[...]).astype(BF)
    gradients("o")
    point()
    pl.loop(0, pairs)(attend_long_back)
    point()
    attend_short_back()
    gradients("q")
    point()
    for j in range(2):
        r.acc_qv[:, j * local : (j + 1) * local] = fold(r.dqkv[:, 2 * j * local : (2 * j + 1) * local].astype(F32))

    def total_of(values):
        return jnp.sum(values, axis=0, keepdims=True)

    r.vec[...] = jnp.zeros_like(r.vec)
    r.vec[0:1, :] = total_of(r.acc_qv[...])
    r.vec[1:2, :] = total_of(r.acc_up[:, :width])
    r.vec[2:3, :] = total_of(r.acc_up[:, width:])
    for j in range(6):
        r.vec[8 + j : 9 + j, :] = total_of(r.acc[j])
    vector_copy(0)

    def input_part(rows):
        return mm_nt(r.dqkv[rows, :], r.wqkv[...])

    for seg in (1, 0):
        index = 6 + seg
        point()
        r.out_buf[index] = input_part(rows_of(peer_start(seg), half)).astype(BF)
        ex[f"dx{seg}"] = remote(r.out_buf.at[index], r.in_buf.at[index], index, peer)
        point()
        r.own[seg] = input_part(rows_of(own_start(seg), half))
    for seg in (1, 0):
        point()
        ex[f"dx{seg}"].wait_recv()
        dfirst = r.ds[seg * half : (seg + 1) * half, :]
        r.dxo[seg] = (dfirst + r.own[seg] + r.in_buf[6 + seg].astype(F32)).astype(BF)
        publish(3, seg, r.dxs, r.dxl, r.dxo)
    if reduce_here:
        while todo:
            handle()
    else:
        for c in range(CHUNKS):
            cp = pltpu.make_async_copy(
                getattr(r, f"G{c}"), r.grads.at[:, :, pl.ds(COLUMNS[c], COLUMNS[c + 1] - COLUMNS[c])], r.out_sem.at[6]
            )
            cp.start()
            cp.wait()
        vector_advance()
    r.sums[...] = r.vec[...]

    for cp in outs:
        cp.wait()
    for cp in arrivals:
        cp.wait_recv()
    for cp in sends:
        cp.wait_send()


COLUMNS = (
    0, 256, 512, 768, 1024, 1280, 1536, 1792, 2048, 2304, 2560, 2816, 3072, 3200, 3328, 3456, 3584, 3712, 3840,
    3968, 4096, 4224, 4352, 4480, 4608,
)
KINDS = (
    11, 13, 3, 11, 3, 14, 7, 7, 7, 4, 8, 7, 0, 3, 14, 8, 6, 3, 8, 6, 6, 0, 2, 0,
)
CHUNKS = len(KINDS)
JOBS = (
    ("d", 0, 1),
    ("d", 1, 2),
    ("d", 2, 4),
    ("d", 4, 6),
    ("u", 6, 8),
    ("u", 8, 10),
    ("u", 10, 12),
    ("o", 12, 15),
    ("q", 15, 24),
)
EVENTS = (
    0, 2, 3, 1, 4, 6, 9, 7, 2, 0, 8, 1, 4, 13, 10, 3, 6, 17, 7, 15, 8, 24, 11, 22, 13, 18, 16, 17, 10, 6, 24, 7,
    19, 5, 11, 15, 16, 18, 8, 20, 12, 10, 24, 0, 14, 19, 3, 15, 21, 5, 16, 18, 11, 23, 20, 24, 9, 14, 12, 19,
    22, 21, 2, 5, 1, 23, 4, 20, 14, 13, 17, 9, 12, 22, 21, 23, 6, 7, 8, 0, 10, 3, 15, 16, 11, 18, 24, 19, 2, 1,
    5, 4, 13, 20, 17, 9, 14, 12, 22, 21, 23,
)
MARKS = (
    0, 0, 0, 0, 0, 0, 0, 0, 0, 0, 0, 0, 0, 0, 1, 1, 1, 2, 2, 3, 4, 5, 5, 7, 7, 10, 13, 14, 14, 15, 15, 16, 17,
    17,
)
EARLY = 5


def shards(n_dp, *args):
    (
        xs, xl, wq, qb, wk, wv, vb, wo, ob, g1, b1, wu, ub, wd, db, g2, b2, us, ul, sl, ll, live,
    ) = args
    short_slots, short_length, width = xs.shape
    long_length = xl.shape[1]
    local, hidden = wq.shape[1], wu.shape[1]
    heads = local // HEAD
    rows = short_slots * short_length + xl.shape[0] * long_length
    half = long_length // 2
    reduce_here = n_dp == 1 << BITS
    blocks = 1 << BITS
    block = width // blocks
    columns = 4 * local + 2 * hidden
    spans = [COLUMNS[c + 1] - COLUMNS[c] for c in range(CHUNKS)]
    assert COLUMNS[-1] == columns
    any_spec = pl.BlockSpec(memory_space=pl.ANY)
    vmem = pl.BlockSpec(memory_space=pltpu.VMEM)
    smem = pl.BlockSpec(memory_space=pltpu.SMEM)
    inputs = [
        ("sl", sl, smem), ("ll", ll, smem), ("live", live, smem),
        ("xs", xs, any_spec), ("xl", xl, any_spec), ("us", us, any_spec), ("ul", ul, any_spec),
        ("wq_h", wq, any_spec), ("wk_h", wk, any_spec), ("wv_h", wv, any_spec), ("wo_h", wo, any_spec),
        ("wu_h", wu, any_spec), ("wd_h", wd, any_spec),
        ("qb", qb, vmem), ("vb", vb, vmem), ("ob", ob, vmem), ("g1", g1, vmem), ("b1", b1, vmem),
        ("ub", ub, vmem), ("db", db, vmem), ("g2", g2, vmem), ("b2", b2, vmem),
    ]
    sds = jax.ShapeDtypeStruct
    outputs = [
        ("os", sds(xs.shape, BF), any_spec), ("ol", sds(xl.shape, BF), any_spec),
        ("dxs", sds(xs.shape, BF), any_spec), ("dxl", sds(xl.shape, BF), any_spec),
    ]
    if reduce_here:
        outputs.append(("rows", sds((block, columns), F32), any_spec))
    else:
        outputs.append(("grads", sds((blocks, block, columns), BF), any_spec))
    outputs.append(("sums", sds((16, width), F32), vmem))
    v = pltpu.VMEM
    dma = pltpu.SemaphoreType.DMA
    scratch = [
        ("x", v((rows, width), BF)), ("ups", v((short_slots // 2, short_length, width), BF)), ("upl", v((half, width), BF)),
        ("wqkv", v((width, 3 * local), BF)), ("wo", v(wo.shape, BF)),
        ("wu", v(wu.shape, BF)), ("wd", v(wd.shape, BF)),
        ("qkv", v((rows, 3 * local), BF)),
        ("pl", v((heads, long_length, long_length), BF)), ("ps", v((short_slots, heads, short_length, short_length), BF)),
        ("ctx", v((rows, local), BF)), ("n1", v((2 * half, width), F32)), ("r1", v((2 * half, 1), F32)),
        ("h", v((rows, width), BF)), ("f", v((rows, hidden), BF)), ("gp", v((rows, hidden), BF)),
        ("do", v((rows, width), BF)), ("ds", v((2 * half, width), F32)), ("da", v((rows, width), BF)),
        ("dctx", v((rows, local), BF)), ("dqkv", v((rows, 3 * local), BF)),
        ("own", v((2, half, width), F32)), ("out_buf", v((8, half, width), BF)), ("in_buf", v((8, half, width), BF)),
        ("out", v((2, half, width), BF)), ("dxo", v((2, half, width), BF)),
        ("acc", v((6, 8, width), F32)), ("acc_up", v((8, hidden), F32)), ("acc_qv", v((8, 2 * local), F32)),
        ("vec", v((16, width), F32)), ("vec_out", v((5, 16, width), BF)), ("vec_in", v((5, 16, width), BF)),
        ("load_sem", dma((16,))), ("out_sem", dma((8,))), ("ex_send", dma((28,))), ("ex_recv", dma((28,))),
        ("held_rows", v((block, columns), F32)), ("row_sem", dma((len(spans),))),
        ("rs_send", dma((len(spans), BITS))), ("rs_recv", dma((len(spans), BITS))),
    ]
    for c, span in enumerate(spans):
        scratch.append((f"G{c}", v((blocks, block, span), BF)))
        scratch.append((f"R{c}", v((blocks - 1 if reduce_here else 1, block, span), BF)))
    names = [n for n, *_ in inputs] + [n for n, *_ in outputs] + [n for n, *_ in scratch]
    macs = rows * width * (8 * local + 6 * hidden)
    results = pl.pallas_call(
        functools.partial(layer, reduce_here, names),
        out_shape=[o[1] for o in outputs],
        in_specs=[i[2] for i in inputs],
        out_specs=[o[2] for o in outputs],
        scratch_shapes=[s[1] for s in scratch],
        cost_estimate=pl.CostEstimate(flops=2 * macs, bytes_accessed=20 << 20, transcendentals=0),
        compiler_params=pltpu.CompilerParams(
            collective_id=0, has_side_effects=True, vmem_limit_bytes=62 << 20
        ),
    )(*[i[1] for i in inputs])
    got = dict(zip([o[0] for o in outputs], results, strict=True))
    if not reduce_here:
        grads = got["grads"].reshape(width, columns).astype(F32)
        got["rows"] = lax.psum_scatter(grads, "dp", scatter_dimension=0, tiled=True)
        got["sums"] = lax.psum(got["sums"], "dp")
    block = width // n_dp
    finals = [
        ("os", sds(xs.shape, BF), any_spec), ("ol", sds(xl.shape, BF), any_spec),
        ("dxs", sds(xs.shape, BF), any_spec), ("dxl", sds(xl.shape, BF), any_spec),
        ("gq", sds((block, local), F32), any_spec), ("g_qb", sds((local // n_dp,), F32), vmem),
        ("gk", sds((block, local), F32), any_spec), ("gv", sds((block, local), F32), any_spec),
        ("g_vb", sds((local // n_dp,), F32), vmem), ("gout", sds((block, local), F32), any_spec),
        ("g_ob", sds((block,), F32), vmem), ("g_gain1", sds((block,), F32), vmem), ("g_shift1", sds((block,), F32), vmem),
        ("gup", sds((block, hidden), F32), any_spec), ("g_ub", sds((hidden // n_dp,), F32), vmem),
        ("gdown", sds((block, hidden), F32), any_spec),
        ("g_db", sds((block,), F32), vmem), ("g_gain2", sds((block,), F32), vmem), ("g_shift2", sds((block,), F32), vmem),
    ]
    sources = ("os", "ol", "dxs", "dxl", "rows", "sums")
    names = ["in_" + n for n in sources] + [f[0] for f in finals] + ["held_" + n for n in sources[:5]] + ["into", "out"]
    results = pl.pallas_call(
        functools.partial(place_results, n_dp, names),
        out_shape=[f[1] for f in finals],
        in_specs=[any_spec] * 5 + [vmem],
        out_specs=[f[2] for f in finals],
        scratch_shapes=[v(got[n].shape, got[n].dtype) for n in sources[:5]] + [dma((10,)), dma((10,))],
        cost_estimate=pl.CostEstimate(flops=0, bytes_accessed=8 << 20, transcendentals=0),
        compiler_params=pltpu.CompilerParams(vmem_limit_bytes=62 << 20),
    )(*[got[n] for n in sources])
    return tuple(result.T if f[0] in ("gout", "gdown") else result for f, result in zip(finals, results, strict=True))


def place_results(n_dp, names, *refs):
    r = Refs()
    for name, ref in zip(names, refs, strict=True):
        setattr(r, name, ref)
    moves = []
    at = 0
    for ref in (r.gdown, r.gup, r.gout, r.gq, r.gk, r.gv):
        cols = slice(at, at + ref.shape[1])
        moves.append((r.in_rows.at[:, cols], r.held_rows.at[:, cols], ref))
        at += ref.shape[1]
    moves += [(getattr(r, "in_" + n), getattr(r, "held_" + n), getattr(r, n)) for n in ("os", "ol", "dxs", "dxl")]
    into = [pltpu.make_async_copy(source, held, r.into.at[j]) for j, (source, held, _) in enumerate(moves)]
    out = [pltpu.make_async_copy(held, target, r.out.at[j]) for j, (_, held, target) in enumerate(moves)]
    for cp in into:
        cp.start()
    for cp, back in zip(into, out):
        cp.wait()
        back.start()
    dp = lax.axis_index("dp")
    local = r.gq.shape[1]
    width = r.in_sums.shape[1]

    def turn(start):
        return pltpu.roll(r.in_sums[...], lax.rem(2 * width - start, width), 1)

    size = r.g_ob.shape[0]
    turned = turn(dp * size)
    for j, ref in enumerate((r.g_gain2, r.g_shift2, r.g_db, r.g_gain1, r.g_shift1, r.g_ob)):
        ref[...] = turned[8 + j : 9 + j, :size].reshape(size)
    size = r.g_qb.shape[0]
    turned = turn(dp * size)
    r.g_qb[...] = turned[0:1, :size].reshape(size)
    r.g_vb[...] = turned[0:1, local : local + size].reshape(size)
    size = r.g_ub.shape[0]
    turned = turn(lax.rem(dp * size, width))
    r.g_ub[...] = jnp.where(dp * size < width, turned[1:2, :size], turned[2:3, :size]).reshape(size)
    for cp in out:
        cp.wait()


def solution(mesh):
    in_specs = (
        P("dp", None, None), P("dp", None, None), P(None, "mp"), P("mp"), P(None, "mp"), P(None, "mp"), P("mp"),
        P("mp", None), P(), P(), P(), P(None, "mp"), P("mp"), P("mp", None), P(), P(), P(),
        P("dp", None, None), P("dp", None, None), P("dp"), P("dp"), P("dp", None),
    )
    out_specs = (
        P("dp", None, None), P("dp", None, None), P("dp", None, None), P("dp", None, None),
        P("dp", "mp"), P(("mp", "dp")), P("dp", "mp"), P("dp", "mp"), P(("mp", "dp")), P("mp", "dp"),
        P("dp"), P("dp"), P("dp"), P("dp", "mp"), P(("mp", "dp")), P("mp", "dp"), P("dp"), P("dp"), P("dp"),
    )
    return jax.shard_map(
        functools.partial(shards, mesh.shape["dp"]),
        mesh=mesh, in_specs=in_specs, out_specs=out_specs, check_vma=False,
    )
```

```python
import functools

import jax
import jax.numpy as jnp
from jax import lax
from jax.experimental import pallas as pl
from jax.experimental.pallas import tpu as pltpu
from jax.sharding import PartitionSpec as P

HEAD = 64
PAIR = 2 * HEAD
NEGATIVE = -1e30
EPSILON = 1e-12
BF = jnp.bfloat16
F32 = jnp.float32
MESH = pl.DeviceIdType.MESH

BITS = 4
X, Y, NEAR, FAR = 0, 1, 2, 3
ORDERS = (
    (X, Y, NEAR, FAR),
    (X, Y, FAR, NEAR),
    (X, NEAR, Y, FAR),
    (X, NEAR, FAR, Y),
    (X, FAR, Y, NEAR),
    (X, FAR, NEAR, Y),
    (Y, X, NEAR, FAR),
    (Y, X, FAR, NEAR),
    (Y, NEAR, X, FAR),
    (Y, NEAR, FAR, X),
    (Y, FAR, X, NEAR),
    (Y, FAR, NEAR, X),
    (NEAR, X, Y, FAR),
    (NEAR, X, FAR, Y),
    (NEAR, Y, X, FAR),
    (NEAR, Y, FAR, X),
    (NEAR, FAR, X, Y),
    (NEAR, FAR, Y, X),
)
PARTS_AT = (0, 8, 12, 14)


def mm(left, right):
    return jnp.dot(left, right, preferred_element_type=F32)


def mm_nt(left, right):
    return lax.dot_general(left, right, (((1,), (1,)), ((), ())), preferred_element_type=F32)


def mm_tn(left, right):
    return lax.dot_general(left, right, (((0,), (0,)), ((), ())), preferred_element_type=F32)


def rows_of(start, size):
    return pl.ds(pl.multiple_of(start, size), size)


def fold(values):
    rows, width = values.shape
    return jnp.sum(values.reshape(rows // 8, 8, width), axis=0)


def place(order, block):
    spot = 0
    for bit in order:
        spot = spot * 2 + ((block >> bit) & 1)
    return spot


class Refs:
    pass


def layer(reduce_here, names, *refs):
    r = Refs()
    for name, ref in zip(names, refs, strict=True):
        setattr(r, name, ref)
    dp, mp = lax.axis_index("dp"), lax.axis_index("mp")
    peer = (dp, 1 - mp)
    half = r.own.shape[1]
    seg_rows = 2 * half
    width = r.x.shape[1]
    local = r.ctx.shape[1]
    pairs = local // PAIR
    heads = local // HEAD
    hidden = r.f.shape[1]
    short_slots, short_length = r.xs.shape[0], r.xs.shape[1]
    long_length = r.xl.shape[1]
    block = r.G0.shape[1]
    tile = 64

    my_bit = [lax.rem(lax.div(dp, 1 << k), 2) for k in range(BITS)]
    across = [(dp + (1 - 2 * my_bit[k]) * (1 << k), mp) for k in range(BITS)]

    barrier = pltpu.get_barrier_semaphore()
    partners = [peer] + (across if reduce_here else [])
    for other in partners:
        pl.semaphore_signal(barrier, inc=1, device_id=other, device_id_type=MESH)

    loads = {}

    def load(name, src, dst):
        cp = pltpu.make_async_copy(src, dst, r.load_sem.at[len(loads)])
        cp.start()
        loads[name] = cp

    load("xl", r.xl.at[0], r.x.at[pl.ds(seg_rows, seg_rows)])
    for j, source in enumerate((r.wq_h, r.wk_h, r.wv_h)):
        load(f"w{j}", source, r.wqkv.at[:, pl.ds(j * local, local)])

    def load_rest():
        for s in range(short_slots):
            load(f"xs{s}", r.xs.at[s], r.x.at[pl.ds(s * short_length, short_length)])
        load("wo", r.wo_h, r.wo)
        load("wu", r.wu_h, r.wu)
        load("wd", r.wd_h, r.wd)
        load("us", r.us.at[pl.ds(mp * (short_slots // 2), short_slots // 2)], r.ups)
        load("ul", r.ul.at[0, rows_of(mp * half, half)], r.upl)

    sends = []

    def remote(src, dst, index, device):
        cp = pltpu.make_async_remote_copy(
            src_ref=src,
            dst_ref=dst,
            send_sem=r.ex_send.at[index],
            recv_sem=r.ex_recv.at[index],
            device_id=device,
            device_id_type=MESH,
        )
        cp.start()
        sends.append(cp)
        return cp

    live_short, live_long = r.live[0, 0], r.live[0, 1]
    long_len = jnp.where(live_long > 0, r.ll[0], 0)

    def short_len(slot):
        return jnp.where(slot < live_short, r.sl[slot], 0)

    def param(ref):
        return ref[...].astype(F32).reshape(1, -1)

    qb, vb, ob, g1, b1 = (param(n) for n in (r.qb, r.vb, r.ob, r.g1, r.b1))
    ub, db, g2, b2 = (param(n) for n in (r.ub, r.db, r.g2, r.b2))

    low_lane = lax.broadcasted_iota(jnp.int32, (1, PAIR), 1) < HEAD

    def first(values):
        return jnp.where(low_lane, values, jnp.zeros_like(values))

    def second(values):
        return jnp.where(low_lane, jnp.zeros_like(values), values)

    def own_start(seg):
        return seg * seg_rows + mp * half

    def peer_start(seg):
        return seg * seg_rows + (1 - mp) * half

    r.acc[...] = jnp.zeros_like(r.acc)
    r.acc_up[...] = jnp.zeros_like(r.acc_up)
    r.acc_qv[...] = jnp.zeros_like(r.acc_qv)

    def project(seg):
        rows = slice(seg * seg_rows, (seg + 1) * seg_rows)
        product = mm(r.x[rows, :], r.wqkv[...])
        r.qkv[rows, :local] = (product[:, :local] + qb).astype(BF) * BF(HEAD**-0.5)
        r.qkv[rows, local : 2 * local] = product[:, local : 2 * local].astype(BF)
        r.qkv[rows, 2 * local :] = (product[:, 2 * local :] + vb).astype(BF)

    def softmax(scores):
        highest = [jnp.max(s, axis=-1, keepdims=True) for s in scores]
        expo = [jnp.exp(s - m) for s, m in zip(scores, highest)]
        total = [1.0 / jnp.sum(e, axis=-1, keepdims=True) for e in expo]
        return [(e * t).astype(BF) for e, t in zip(expo, total)]

    def lanes_of(pair, part=0):
        if isinstance(pair, int):
            return slice(part * local + pair * PAIR, part * local + (pair + 1) * PAIR)
        return rows_of(part * local + pair * PAIR, PAIR)

    def parts_of(ref, rows, pair):
        return [ref[rows, lanes_of(pair, part)] for part in range(3)]

    def slot_rows(s):
        return slice(s * short_length, (s + 1) * short_length)

    long_rows = slice(seg_rows, 2 * seg_rows)

    def attend_long():
        position = lax.broadcasted_iota(jnp.int32, (1, long_length), 1)
        bias = jnp.where(position < long_len, 0.0, NEGATIVE)
        for pair in range(pairs):
            qp, kp, vp = parts_of(r.qkv, long_rows, pair)
            parts = []
            for j, pick in enumerate((first, second)):
                (probs,) = softmax([mm_nt(pick(qp), kp) + bias])
                r.pl[2 * pair + j] = probs
                parts.append(mm(probs, vp))
            r.ctx[long_rows, lanes_of(pair)] = jnp.where(low_lane, *parts).astype(BF)

    def attend_short():
        position = lax.broadcasted_iota(jnp.int32, (1, short_length), 1)
        scores = []
        for s in range(short_slots):
            bias = jnp.where(position < short_len(s), 0.0, NEGATIVE)
            for pair in range(pairs):
                qp, kp, _ = parts_of(r.qkv, slot_rows(s), pair)
                scores += [mm_nt(first(qp), kp) + bias, mm_nt(second(qp), kp) + bias]
        probs = softmax(scores)
        for s in range(short_slots):
            for pair in range(pairs):
                parts = []
                for head in (2 * pair, 2 * pair + 1):
                    r.ps[s, head] = probs[s * heads + head]
                    parts.append(mm(probs[s * heads + head], r.qkv[slot_rows(s), lanes_of(pair, 2)]))
                r.ctx[slot_rows(s), lanes_of(pair)] = jnp.where(low_lane, *parts).astype(BF)

    def exchange(stage, seg, left, right, product, between=lambda: None):
        index = 2 * stage + seg
        r.out_buf[index] = product(left[rows_of(peer_start(seg), half), :], right[...]).astype(BF)
        cp = remote(r.out_buf.at[index], r.in_buf.at[index], index, peer)
        between()
        r.own[seg] = product(left[rows_of(own_start(seg), half), :], right[...])
        return cp

    def share(index, seg, ref):
        rows = rows_of(own_start(seg), half)
        return remote(ref.at[rows], ref.at[rows], index, peer)

    def norm(values):
        mean = jnp.mean(values, axis=-1, keepdims=True)
        centred = values - mean
        scale = lax.rsqrt(jnp.mean(centred * centred, axis=-1, keepdims=True) + EPSILON)
        return centred * scale, scale

    def norm_back(normed, scale, grad):
        return scale * (
            grad
            - jnp.mean(grad, axis=-1, keepdims=True)
            - normed * jnp.mean(grad * normed, axis=-1, keepdims=True)
        )

    def norm_one(seg):
        for t in range(half // tile):
            mine = slice(seg * half + t * tile, seg * half + (t + 1) * tile)
            here = slice(t * tile, (t + 1) * tile)
            rows = rows_of(own_start(seg) + t * tile, tile)
            total = r.own[seg, here, :] + r.in_buf[seg, here, :].astype(F32) + ob
            normed, scale = norm(r.x[rows, :].astype(F32) + total)
            r.n1[mine, :] = normed
            r.r1[mine, :] = scale
            r.h[rows, :] = (normed * g1 + b1).astype(BF)

    def up(start):
        rows = rows_of(start, half)
        step = 256
        for j in range(hidden // step):
            cols = slice(j * step, (j + 1) * step)
            pre = mm(r.h[rows, :], r.wu[:, cols]) + ub[:, cols]
            phi = 0.5 + 0.5 * lax.erf(pre * (0.5**0.5))
            r.f[rows, cols] = (pre * phi).astype(BF)
            r.gp[rows, cols] = (phi + pre * (jnp.exp(pre * pre * -0.5) * 0.3989422804014327)).astype(BF)

    def norm_two(seg):
        for t in range(half // tile):
            mine = slice(seg * half + t * tile, seg * half + (t + 1) * tile)
            here = slice(t * tile, (t + 1) * tile)
            rows = rows_of(own_start(seg) + t * tile, tile)
            row = lax.broadcasted_iota(jnp.int32, (tile, 1), 0)
            if seg == 0:
                slot, inner = t * tile // short_length, t * tile % short_length
                keep = row + inner < short_len(mp * (short_slots // 2) + slot)
                upstream = r.ups[slot, inner : inner + tile, :]
            else:
                keep = row + (mp * half + t * tile) < long_len
                upstream = r.upl[here, :]
            keep = keep.astype(F32)
            hidden_state = r.n1[mine, :] * g1 + b1
            total = r.own[seg, here, :] + r.in_buf[2 + seg, here, :].astype(F32) + db
            normed, scale = norm(hidden_state + total)
            r.out[seg, here, :] = (keep * (normed * g2 + b2)).astype(BF)
            grad = keep * upstream.astype(F32)
            r.acc[0] += fold(grad * normed)
            r.acc[1] += fold(grad)
            dsecond = norm_back(normed, scale, grad * g2)
            low = dsecond.astype(BF)
            r.acc[2] += fold(low.astype(F32))
            r.ds[mine, :] = dsecond
            r.do[rows, :] = low

    def norm_one_back(seg):
        for t in range(half // tile):
            mine = slice(seg * half + t * tile, seg * half + (t + 1) * tile)
            here = slice(t * tile, (t + 1) * tile)
            rows = rows_of(own_start(seg) + t * tile, tile)
            grad = r.ds[mine, :] + r.own[seg, here, :] + r.in_buf[4 + seg, here, :].astype(F32)
            normed = r.n1[mine, :]
            r.acc[3] += fold(grad * normed)
            r.acc[4] += fold(grad)
            dfirst = norm_back(normed, r.r1[mine, :], grad * g1)
            low = dfirst.astype(BF)
            r.acc[5] += fold(low.astype(F32))
            r.ds[mine, :] = dfirst
            r.da[rows, :] = low

    def active_back(seg):
        for part in range(2):
            rows = slice(seg * seg_rows + part * half, seg * seg_rows + (part + 1) * half)
            step = 512
            for j in range(hidden // step):
                cols = slice(j * step, (j + 1) * step)
                low = (mm_nt(r.do[rows, :], r.wd[cols, :]) * r.gp[rows, cols].astype(F32)).astype(BF)
                r.acc_up[:, cols] += fold(low.astype(F32))
                r.gp[rows, cols] = low
                yield

    def dscores(rows, pair, probs):
        vp, dc = r.qkv[rows, lanes_of(pair, 2)], r.dctx[rows, lanes_of(pair)]
        product = dc.astype(F32) * r.ctx[rows, lanes_of(pair)].astype(F32)
        held = []
        for j, pick in enumerate((first, second)):
            inner = jnp.sum(pick(product), axis=-1, keepdims=True)
            held.append((probs[j].astype(F32) * (mm_nt(pick(dc), vp) - inner)).astype(BF))
        return held

    def heads_back(rows, pair, probs, held):
        qp, kp, _ = parts_of(r.qkv, rows, pair)
        dc = r.dctx[rows, lanes_of(pair)]
        dq = jnp.where(low_lane, mm(held[0], kp), mm(held[1], kp)) * HEAD**-0.5
        r.dqkv[rows, lanes_of(pair)] = dq.astype(BF)
        r.dqkv[rows, lanes_of(pair, 1)] = jnp.where(low_lane, mm_tn(held[0], qp), mm_tn(held[1], qp)).astype(BF)
        r.dqkv[rows, lanes_of(pair, 2)] = jnp.where(low_lane, mm_tn(probs[0], dc), mm_tn(probs[1], dc)).astype(BF)

    def attend_long_back(pair):
        probs = [r.pl[2 * pair], r.pl[2 * pair + 1]]
        heads_back(long_rows, pair, probs, dscores(long_rows, pair, probs))

    def attend_short_back():
        each = [(s, pair) for s in range(short_slots) for pair in range(pairs)]
        probs = [[r.ps[s, 2 * pair], r.ps[s, 2 * pair + 1]] for s, pair in each]
        held = [dscores(slot_rows(s), pair, p) for (s, pair), p in zip(each, probs)]
        for (s, pair), p, h in zip(each, probs, held):
            heads_back(slot_rows(s), pair, p, h)

    begin, flight = {}, {}

    def half_copy(c, p):
        n = 8 >> p
        bit = ORDERS[KINDS[c]][p]
        start = begin.get(c, 0)
        held, landed = getattr(r, f"G{c}"), getattr(r, f"R{c}")
        cp = pltpu.make_async_remote_copy(
            src_ref=held.at[pl.ds(start + (1 - my_bit[bit]) * n, n)],
            dst_ref=landed.at[pl.ds(PARTS_AT[p], n)],
            send_sem=r.rs_send.at[c, p],
            recv_sem=r.rs_recv.at[c, p],
            device_id=across[bit],
            device_id_type=MESH,
        )
        cp.start()
        sends.append(cp)
        begin[c] = start + my_bit[bit] * n
        flight[c] = (p, cp)

    def operands(start, stop):
        for left, right in ((r.do, r.f), (r.h, r.gp), (r.da, r.ctx), (r.x, r.dqkv)):
            span = right.shape[1]
            if start < span:
                return left, right, slice(start, stop)
            start, stop = start - span, stop - span

    def gradient(begins, ends):
        blocks = 1 << BITS
        part = width // 2
        base = COLUMNS[begins]
        left, right, cols = operands(base, COLUMNS[ends])
        orders = [ORDERS[KINDS[c]] if reduce_here else (3, 2, 1, 0) for c in range(begins, ends)]

        @pl.loop(0, 2)
        def _(m):
            piece = mm_tn(left[:, rows_of(m * part, part)], right[:, cols]).astype(BF)
            for c, order in zip(range(begins, ends), orders):
                held = getattr(r, f"G{c}")
                own = piece[:, COLUMNS[c] - base : COLUMNS[c + 1] - base]
                for b in range(blocks // 2):
                    held[place(order, b) + m * place(order, blocks // 2)] = own[b * block : (b + 1) * block]

        if reduce_here:
            for c in range(begins, ends):
                half_copy(c, 0)

    vector = [None, 0]

    def vector_copy(k):
        r.vec_out[k] = r.vec[...].astype(BF)
        device = peer if k == 0 else across[k - 1]
        vector[:] = remote(r.vec_out.at[k], r.vec_in.at[k], 22 + k, device), k

    def vector_advance():
        cp, k = vector
        cp.wait_recv()
        rows = slice(8 if k == 0 else 0, 16)
        r.vec[rows, :] = (r.vec_out[k].astype(F32) + r.vec_in[k].astype(F32))[rows]
        if k < BITS and reduce_here:
            vector_copy(k + 1)
        else:
            cp = pltpu.make_async_copy(r.vec, r.sums, r.out_sem.at[7])
            cp.start()
            outs.append(cp)

    def advance(c):
        p, cp = flight.pop(c)
        n = 8 >> p
        held, landed = getattr(r, f"G{c}"), getattr(r, f"R{c}")
        cp.wait_recv()
        if p < BITS - 1:
            mine = pl.ds(begin[c], n)
            held[mine] = held[mine] + landed[PARTS_AT[p] : PARTS_AT[p] + n]
            half_copy(c, p + 1)
        else:
            total = held[begin[c]].astype(F32) + landed[PARTS_AT[p]].astype(F32)
            cols = slice(COLUMNS[c], COLUMNS[c + 1])
            r.held_rows[:, cols] = total
            cp = pltpu.make_async_copy(r.held_rows.at[:, cols], r.rows.at[:, cols], r.row_sem.at[c])
            cp.start()
            outs.append(cp)

    todo = list(EVENTS) if reduce_here else []
    marks = list(MARKS)

    def handle():
        c = todo.pop(0)
        if c < CHUNKS:
            advance(c)
        else:
            vector_advance()

    def point():
        upto = marks.pop(0) if marks else len(EVENTS)
        while todo and len(EVENTS) - len(todo) < upto:
            handle()

    def gradients(group):
        for job, begins, ends in JOBS:
            if job == group:
                point()
                gradient(begins, ends)

    for name in ("xl", "w0", "w1", "w2"):
        loads[name].wait()
    load_rest()
    project(1)
    attend_long()
    for s in range(short_slots):
        loads[f"xs{s}"].wait()
    project(0)
    loads["wo"].wait()
    pl.semaphore_wait(barrier, len(partners))
    ex = {}
    ex["a1"] = exchange(0, 1, r.ctx, r.wo, mm)
    attend_short()
    ex["a1"].wait_recv()
    norm_one(1)
    ex["h1"] = share(8, 1, r.h)
    ex["a0"] = exchange(0, 0, r.ctx, r.wo, mm)
    loads["wu"].wait()
    loads["wd"].wait()
    up(own_start(1))
    ex["h1"].wait_recv()
    up(peer_start(1))
    ex["a0"].wait_recv()
    norm_one(0)
    ex["h0"] = share(9, 0, r.h)
    ex["o1"] = exchange(1, 1, r.f, r.wd, mm)
    up(own_start(0))
    ex["h0"].wait_recv()
    up(peer_start(0))
    ex["o0"] = exchange(1, 0, r.f, r.wd, mm)
    loads["us"].wait()
    loads["ul"].wait()
    outs, arrivals = [], []

    def publish(index, seg, short_ref, long_ref, held):
        if seg == 0:
            for s in range(short_slots // 2):
                piece = held.at[0, pl.ds(s * short_length, short_length)]
                target = short_ref.at[mp * (short_slots // 2) + s]
                cp = pltpu.make_async_copy(piece, target, r.out_sem.at[index + s])
                cp.start()
                outs.append(cp)
                arrivals.append(remote(piece, target, 16 + index + s, peer))
        else:
            target = long_ref.at[0, rows_of(mp * half, half)]
            cp = pltpu.make_async_copy(held.at[1], target, r.out_sem.at[index + 2])
            cp.start()
            outs.append(cp)
            arrivals.append(remote(held.at[1], target, 16 + index + 2, peer))

    for seg in (1, 0):
        ex[f"o{seg}"].wait_recv()
        norm_two(seg)
        ex[f"do{seg}"] = share(10 + seg, seg, r.do)
    ex["do1"].wait_recv()

    early, late = active_back(1), active_back(0)
    for _ in range(EARLY):
        next(early)
    ex["do0"].wait_recv()
    gradients("d")
    point()
    publish(0, 1, r.os, r.ol, r.out)
    publish(0, 0, r.os, r.ol, r.out)
    for pieces in (early, late):
        for _ in pieces:
            point()
    gradients("u")
    for seg in (1, 0):
        point()
        ex[f"dh{seg}"] = exchange(2, seg, r.gp, r.wu, mm_nt, point)
    for seg in (1, 0):
        point()
        ex[f"dh{seg}"].wait_recv()
        norm_one_back(seg)
        ex[f"da{seg}"] = share(12 + seg, seg, r.da)
    for seg in (1, 0):
        point()
        ex[f"da{seg}"].wait_recv()
        rows = slice(seg * seg_rows, (seg + 1) * seg_rows)
        r.dctx[rows, :] = mm_nt(r.da[rows, :], r.wo[...]).astype(BF)
    gradients("o")
    point()
    pl.loop(0, pairs)(attend_long_back)
    point()
    attend_short_back()
    gradients("q")
    point()
    for j in range(2):
        r.acc_qv[:, j * local : (j + 1) * local] = fold(r.dqkv[:, 2 * j * local : (2 * j + 1) * local].astype(F32))

    def total_of(values):
        return jnp.sum(values, axis=0, keepdims=True)

    r.vec[...] = jnp.zeros_like(r.vec)
    r.vec[0:1, :] = total_of(r.acc_qv[...])
    r.vec[1:2, :] = total_of(r.acc_up[:, :width])
    r.vec[2:3, :] = total_of(r.acc_up[:, width:])
    for j in range(6):
        r.vec[8 + j : 9 + j, :] = total_of(r.acc[j])
    vector_copy(0)

    def input_part(rows):
        return mm_nt(r.dqkv[rows, :], r.wqkv[...])

    for seg in (1, 0):
        index = 6 + seg
        point()
        r.out_buf[index] = input_part(rows_of(peer_start(seg), half)).astype(BF)
        ex[f"dx{seg}"] = remote(r.out_buf.at[index], r.in_buf.at[index], index, peer)
        point()
        r.own[seg] = input_part(rows_of(own_start(seg), half))
    for seg in (1, 0):
        point()
        ex[f"dx{seg}"].wait_recv()
        dfirst = r.ds[seg * half : (seg + 1) * half, :]
        r.dxo[seg] = (dfirst + r.own[seg] + r.in_buf[6 + seg].astype(F32)).astype(BF)
        publish(3, seg, r.dxs, r.dxl, r.dxo)
    if reduce_here:
        while todo:
            handle()
    else:
        for c in range(CHUNKS):
            cp = pltpu.make_async_copy(
                getattr(r, f"G{c}"), r.grads.at[:, :, pl.ds(COLUMNS[c], COLUMNS[c + 1] - COLUMNS[c])], r.out_sem.at[6]
            )
            cp.start()
            cp.wait()
        vector_advance()

    for cp in outs:
        cp.wait()
    for cp in arrivals:
        cp.wait_recv()
    for cp in sends:
        cp.wait_send()


COLUMNS = (
    0, 128, 256, 384, 512, 768, 1024, 1280, 1536, 1792, 2048, 2304, 2560, 2816, 3072, 3328, 3456, 3712, 3968,
    4224, 4352, 4480, 4608,
)
KINDS = (
    14, 3, 16, 11, 7, 3, 4, 9, 5, 9, 0, 2, 6, 6, 9, 14, 1, 8, 0, 2, 0, 6,
)
CHUNKS = len(KINDS)
JOBS = (
    ("d", 0, 2),
    ("d", 2, 4),
    ("d", 4, 6),
    ("d", 6, 8),
    ("u", 8, 10),
    ("u", 10, 12),
    ("u", 12, 14),
    ("o", 14, 16),
    ("q", 16, 22),
)
EVENTS = (
    1, 3, 2, 5, 1, 3, 6, 7, 5, 9, 8, 4, 7, 12, 11, 10, 9, 13, 8, 4, 14, 12, 10, 14, 17, 16, 12, 0, 13, 18, 10,
    4, 16, 11, 17, 19, 8, 22, 13, 15, 21, 18, 20, 9, 11, 14, 19, 16, 2, 22, 17, 0, 1, 21, 15, 6, 18, 7, 20, 5,
    3, 19, 2, 22, 0, 21, 15, 20, 22, 6, 12, 4, 10, 8, 13, 9, 14, 16, 11, 1, 17, 7, 3, 5, 18, 2, 19, 0, 21, 15,
    20, 6, 22,
)
MARKS = (
    0, 0, 0, 0, 0, 0, 0, 1, 2, 2, 3, 3, 3, 3, 4, 4, 6, 7, 7, 8, 8, 9, 10, 10, 10, 11, 13, 15, 19, 20, 21, 21,
    21, 22, 23, 23,
)
EARLY = 3


def shards(n_dp, *args):
    (
        xs, xl, wq, qb, wk, wv, vb, wo, ob, g1, b1, wu, ub, wd, db, g2, b2, us, ul, sl, ll, live,
    ) = args
    short_slots, short_length, width = xs.shape
    long_length = xl.shape[1]
    local, hidden = wq.shape[1], wu.shape[1]
    heads = local // HEAD
    rows = short_slots * short_length + xl.shape[0] * long_length
    half = long_length // 2
    reduce_here = n_dp == 1 << BITS
    blocks = 1 << BITS
    block = width // blocks
    columns = 4 * local + 2 * hidden
    spans = [COLUMNS[c + 1] - COLUMNS[c] for c in range(CHUNKS)]
    assert COLUMNS[-1] == columns
    any_spec = pl.BlockSpec(memory_space=pl.ANY)
    vmem = pl.BlockSpec(memory_space=pltpu.VMEM)
    smem = pl.BlockSpec(memory_space=pltpu.SMEM)
    inputs = [
        ("sl", sl, smem), ("ll", ll, smem), ("live", live, smem),
        ("xs", xs, any_spec), ("xl", xl, any_spec), ("us", us, any_spec), ("ul", ul, any_spec),
        ("wq_h", wq, any_spec), ("wk_h", wk, any_spec), ("wv_h", wv, any_spec), ("wo_h", wo, any_spec),
        ("wu_h", wu, any_spec), ("wd_h", wd, any_spec),
        ("qb", qb, vmem), ("vb", vb, vmem), ("ob", ob, vmem), ("g1", g1, vmem), ("b1", b1, vmem),
        ("ub", ub, vmem), ("db", db, vmem), ("g2", g2, vmem), ("b2", b2, vmem),
    ]
    sds = jax.ShapeDtypeStruct
    outputs = [
        ("os", sds(xs.shape, BF), any_spec), ("ol", sds(xl.shape, BF), any_spec),
        ("dxs", sds(xs.shape, BF), any_spec), ("dxl", sds(xl.shape, BF), any_spec),
    ]
    if reduce_here:
        outputs.append(("rows", sds((block, columns), F32), any_spec))
    else:
        outputs.append(("grads", sds((blocks, block, columns), BF), any_spec))
    outputs.append(("sums", sds((16, width), F32), any_spec))
    v = pltpu.VMEM
    dma = pltpu.SemaphoreType.DMA
    scratch = [
        ("x", v((rows, width), BF)), ("ups", v((short_slots // 2, short_length, width), BF)), ("upl", v((half, width), BF)),
        ("wqkv", v((width, 3 * local), BF)), ("wo", v(wo.shape, BF)),
        ("wu", v(wu.shape, BF)), ("wd", v(wd.shape, BF)),
        ("qkv", v((rows, 3 * local), BF)),
        ("pl", v((heads, long_length, long_length), BF)), ("ps", v((short_slots, heads, short_length, short_length), BF)),
        ("ctx", v((rows, local), BF)), ("n1", v((2 * half, width), F32)), ("r1", v((2 * half, 1), F32)),
        ("h", v((rows, width), BF)), ("f", v((rows, hidden), BF)), ("gp", v((rows, hidden), BF)),
        ("do", v((rows, width), BF)), ("ds", v((2 * half, width), F32)), ("da", v((rows, width), BF)),
        ("dctx", v((rows, local), BF)), ("dqkv", v((rows, 3 * local), BF)),
        ("own", v((2, half, width), F32)), ("out_buf", v((8, half, width), BF)), ("in_buf", v((8, half, width), BF)),
        ("out", v((2, half, width), BF)), ("dxo", v((2, half, width), BF)),
        ("acc", v((6, 8, width), F32)), ("acc_up", v((8, hidden), F32)), ("acc_qv", v((8, 2 * local), F32)),
        ("vec", v((16, width), F32)), ("vec_out", v((5, 16, width), BF)), ("vec_in", v((5, 16, width), BF)),
        ("load_sem", dma((16,))), ("out_sem", dma((8,))), ("ex_send", dma((28,))), ("ex_recv", dma((28,))),
        ("held_rows", v((block, columns), F32)), ("row_sem", dma((len(spans),))),
        ("rs_send", dma((len(spans), BITS))), ("rs_recv", dma((len(spans), BITS))),
    ]
    for c, span in enumerate(spans):
        scratch.append((f"G{c}", v((blocks, block, span), BF)))
        scratch.append((f"R{c}", v((blocks - 1 if reduce_here else 1, block, span), BF)))
    names = [n for n, *_ in inputs] + [n for n, *_ in outputs] + [n for n, *_ in scratch]
    macs = rows * width * (8 * local + 6 * hidden)
    results = pl.pallas_call(
        functools.partial(layer, reduce_here, names),
        out_shape=[o[1] for o in outputs],
        in_specs=[i[2] for i in inputs],
        out_specs=[o[2] for o in outputs],
        scratch_shapes=[s[1] for s in scratch],
        cost_estimate=pl.CostEstimate(flops=2 * macs, bytes_accessed=20 << 20, transcendentals=0),
        compiler_params=pltpu.CompilerParams(
            collective_id=0, has_side_effects=True, vmem_limit_bytes=62 << 20
        ),
    )(*[i[1] for i in inputs])
    got = dict(zip([o[0] for o in outputs], results, strict=True))
    if not reduce_here:
        grads = got["grads"].reshape(width, columns).astype(F32)
        got["rows"] = lax.psum_scatter(grads, "dp", scatter_dimension=0, tiled=True)
        got["sums"] = lax.psum(got["sums"], "dp")
    block = width // n_dp
    finals = [
        ("os", sds(xs.shape, BF), any_spec), ("ol", sds(xl.shape, BF), any_spec),
        ("dxs", sds(xs.shape, BF), any_spec), ("dxl", sds(xl.shape, BF), any_spec),
        ("gq", sds((block, local), F32), any_spec), ("g_qb", sds((local // n_dp,), F32), vmem),
        ("gk", sds((block, local), F32), any_spec), ("gv", sds((block, local), F32), any_spec),
        ("g_vb", sds((local // n_dp,), F32), vmem), ("gout", sds((block, local), F32), any_spec),
        ("g_ob", sds((block,), F32), vmem), ("g_gain1", sds((block,), F32), vmem), ("g_shift1", sds((block,), F32), vmem),
        ("gup", sds((block, hidden), F32), any_spec), ("g_ub", sds((hidden // n_dp,), F32), vmem),
        ("gdown", sds((block, hidden), F32), any_spec),
        ("g_db", sds((block,), F32), vmem), ("g_gain2", sds((block,), F32), vmem), ("g_shift2", sds((block,), F32), vmem),
    ]
    sources = ("os", "ol", "dxs", "dxl", "rows", "sums")
    names = ["in_" + n for n in sources] + [f[0] for f in finals] + ["held_" + n for n in sources] + ["into", "out"]
    results = pl.pallas_call(
        functools.partial(place_results, n_dp, names),
        out_shape=[f[1] for f in finals],
        in_specs=[any_spec] * 6,
        out_specs=[f[2] for f in finals],
        scratch_shapes=[v(got[n].shape, got[n].dtype) for n in sources] + [dma((11,)), dma((10,))],
        cost_estimate=pl.CostEstimate(flops=0, bytes_accessed=8 << 20, transcendentals=0),
        compiler_params=pltpu.CompilerParams(vmem_limit_bytes=62 << 20),
    )(*[got[n] for n in sources])
    return tuple(result.T if f[0] in ("gout", "gdown") else result for f, result in zip(finals, results, strict=True))


def place_results(n_dp, names, *refs):
    r = Refs()
    for name, ref in zip(names, refs, strict=True):
        setattr(r, name, ref)
    moves = []
    at = 0
    for ref in (r.gdown, r.gup, r.gout, r.gq, r.gk, r.gv):
        cols = slice(at, at + ref.shape[1])
        moves.append((r.in_rows.at[:, cols], r.held_rows.at[:, cols], ref))
        at += ref.shape[1]
    moves += [(getattr(r, "in_" + n), getattr(r, "held_" + n), getattr(r, n)) for n in ("os", "ol", "dxs", "dxl")]
    into = [pltpu.make_async_copy(source, held, r.into.at[j]) for j, (source, held, _) in enumerate(moves)]
    out = [pltpu.make_async_copy(held, target, r.out.at[j]) for j, (_, held, target) in enumerate(moves)]
    vectors = pltpu.make_async_copy(r.in_sums, r.held_sums, r.into.at[10])
    vectors.start()
    for cp in into:
        cp.start()
    vectors.wait()
    vector_results(r)
    for cp, back in zip(into, out):
        cp.wait()
        back.start()
    for cp in out:
        cp.wait()


def vector_results(r):
    dp = lax.axis_index("dp")
    local = r.gq.shape[1]
    width = r.held_sums.shape[1]

    def turn(start):
        return pltpu.roll(r.held_sums[...], lax.rem(2 * width - start, width), 1)

    size = r.g_ob.shape[0]
    turned = turn(dp * size)
    for j, ref in enumerate((r.g_gain2, r.g_shift2, r.g_db, r.g_gain1, r.g_shift1, r.g_ob)):
        ref[...] = turned[8 + j : 9 + j, :size].reshape(size)
    size = r.g_qb.shape[0]
    turned = turn(dp * size)
    r.g_qb[...] = turned[0:1, :size].reshape(size)
    r.g_vb[...] = turned[0:1, local : local + size].reshape(size)
    size = r.g_ub.shape[0]
    turned = turn(lax.rem(dp * size, width))
    r.g_ub[...] = jnp.where(dp * size < width, turned[1:2, :size], turned[2:3, :size]).reshape(size)


def solution(mesh):
    in_specs = (
        P("dp", None, None), P("dp", None, None), P(None, "mp"), P("mp"), P(None, "mp"), P(None, "mp"), P("mp"),
        P("mp", None), P(), P(), P(), P(None, "mp"), P("mp"), P("mp", None), P(), P(), P(),
        P("dp", None, None), P("dp", None, None), P("dp"), P("dp"), P("dp", None),
    )
    out_specs = (
        P("dp", None, None), P("dp", None, None), P("dp", None, None), P("dp", None, None),
        P("dp", "mp"), P(("mp", "dp")), P("dp", "mp"), P("dp", "mp"), P(("mp", "dp")), P("mp", "dp"),
        P("dp"), P("dp"), P("dp"), P("dp", "mp"), P(("mp", "dp")), P("mp", "dp"), P("dp"), P("dp"), P("dp"),
    )
    return jax.shard_map(
        functools.partial(shards, mesh.shape["dp"]),
        mesh=mesh, in_specs=in_specs, out_specs=out_specs, check_vma=False,
    )
```

```python
import functools

import jax
import jax.numpy as jnp
from jax import lax
from jax.experimental import pallas as pl
from jax.experimental.pallas import tpu as pltpu
from jax.sharding import PartitionSpec as P

HEAD = 64
PAIR = 2 * HEAD
NEGATIVE = -1e30
EPSILON = 1e-12
BF = jnp.bfloat16
F32 = jnp.float32
MESH = pl.DeviceIdType.MESH

BITS = 4
X, Y, NEAR, FAR = 0, 1, 2, 3
ORDERS = (
    (X, Y, NEAR, FAR),
    (X, Y, FAR, NEAR),
    (X, NEAR, Y, FAR),
    (X, NEAR, FAR, Y),
    (X, FAR, Y, NEAR),
    (X, FAR, NEAR, Y),
    (Y, X, NEAR, FAR),
    (Y, X, FAR, NEAR),
    (Y, NEAR, X, FAR),
    (Y, NEAR, FAR, X),
    (Y, FAR, X, NEAR),
    (Y, FAR, NEAR, X),
    (NEAR, X, Y, FAR),
    (NEAR, X, FAR, Y),
    (NEAR, Y, X, FAR),
    (NEAR, Y, FAR, X),
    (NEAR, FAR, X, Y),
    (NEAR, FAR, Y, X),
)
PARTS_AT = (0, 8, 12, 14)


def mm(left, right):
    return jnp.dot(left, right, preferred_element_type=F32)


def mm_nt(left, right):
    return lax.dot_general(left, right, (((1,), (1,)), ((), ())), preferred_element_type=F32)


def mm_tn(left, right):
    return lax.dot_general(left, right, (((0,), (0,)), ((), ())), preferred_element_type=F32)


def rows_of(start, size):
    return pl.ds(pl.multiple_of(start, size), size)


def fold(values):
    rows, width = values.shape
    return jnp.sum(values.reshape(rows // 8, 8, width), axis=0)


def place(order, block):
    spot = 0
    for bit in order:
        spot = spot * 2 + ((block >> bit) & 1)
    return spot


class Refs:
    pass


def layer(reduce_here, names, *refs):
    r = Refs()
    for name, ref in zip(names, refs, strict=True):
        setattr(r, name, ref)
    dp, mp = lax.axis_index("dp"), lax.axis_index("mp")
    peer = (dp, 1 - mp)
    half = r.own.shape[1]
    seg_rows = 2 * half
    width = r.x.shape[1]
    local = r.ctx.shape[1]
    pairs = local // PAIR
    heads = local // HEAD
    hidden = r.f.shape[1]
    short_slots, short_length = r.xs.shape[0], r.xs.shape[1]
    long_length = r.xl.shape[1]
    block = r.G0.shape[1]
    tile = 64

    my_bit = [lax.rem(lax.div(dp, 1 << k), 2) for k in range(BITS)]
    across = [(dp + (1 - 2 * my_bit[k]) * (1 << k), mp) for k in range(BITS)]

    barrier = pltpu.get_barrier_semaphore()
    partners = [peer] + (across if reduce_here else [])
    for other in partners:
        pl.semaphore_signal(barrier, inc=1, device_id=other, device_id_type=MESH)

    loads = {}

    def load(name, src, dst):
        cp = pltpu.make_async_copy(src, dst, r.load_sem.at[len(loads)])
        cp.start()
        loads[name] = cp

    load("xl", r.xl.at[0], r.x.at[pl.ds(seg_rows, seg_rows)])
    for j, source in enumerate((r.wq_h, r.wk_h, r.wv_h)):
        load(f"w{j}", source, r.wqkv.at[:, pl.ds(j * local, local)])

    def load_rest():
        for s in range(short_slots):
            load(f"xs{s}", r.xs.at[s], r.x.at[pl.ds(s * short_length, short_length)])
        load("wo", r.wo_h, r.wo)
        load("wu", r.wu_h, r.wu)
        load("wd", r.wd_h, r.wd)
        load("us", r.us.at[pl.ds(mp * (short_slots // 2), short_slots // 2)], r.ups)
        load("ul", r.ul.at[0, rows_of(mp * half, half)], r.upl)

    sends = []

    def remote(src, dst, index, device):
        cp = pltpu.make_async_remote_copy(
            src_ref=src,
            dst_ref=dst,
            send_sem=r.ex_send.at[index],
            recv_sem=r.ex_recv.at[index],
            device_id=device,
            device_id_type=MESH,
        )
        cp.start()
        sends.append(cp)
        return cp

    live_short, live_long = r.live[0, 0], r.live[0, 1]
    long_len = jnp.where(live_long > 0, r.ll[0], 0)

    def short_len(slot):
        return jnp.where(slot < live_short, r.sl[slot], 0)

    def param(ref):
        return ref[...].astype(F32).reshape(1, -1)

    qb, vb, ob, g1, b1 = (param(n) for n in (r.qb, r.vb, r.ob, r.g1, r.b1))
    ub, db, g2, b2 = (param(n) for n in (r.ub, r.db, r.g2, r.b2))

    low_lane = lax.broadcasted_iota(jnp.int32, (1, PAIR), 1) < HEAD

    def first(values):
        return jnp.where(low_lane, values, jnp.zeros_like(values))

    def second(values):
        return jnp.where(low_lane, jnp.zeros_like(values), values)

    def own_start(seg):
        return seg * seg_rows + mp * half

    def peer_start(seg):
        return seg * seg_rows + (1 - mp) * half

    r.acc[...] = jnp.zeros_like(r.acc)
    r.acc_up[...] = jnp.zeros_like(r.acc_up)
    r.acc_qv[...] = jnp.zeros_like(r.acc_qv)

    def project(seg):
        rows = slice(seg * seg_rows, (seg + 1) * seg_rows)
        product = mm(r.x[rows, :], r.wqkv[...])
        r.qkv[rows, :local] = (product[:, :local] + qb).astype(BF) * BF(HEAD**-0.5)
        r.qkv[rows, local : 2 * local] = product[:, local : 2 * local].astype(BF)
        r.qkv[rows, 2 * local :] = (product[:, 2 * local :] + vb).astype(BF)

    def softmax(scores):
        highest = [jnp.max(s, axis=-1, keepdims=True) for s in scores]
        expo = [jnp.exp(s - m) for s, m in zip(scores, highest)]
        total = [1.0 / jnp.sum(e, axis=-1, keepdims=True) for e in expo]
        return [(e * t).astype(BF) for e, t in zip(expo, total)]

    def lanes_of(pair, part=0):
        if isinstance(pair, int):
            return slice(part * local + pair * PAIR, part * local + (pair + 1) * PAIR)
        return rows_of(part * local + pair * PAIR, PAIR)

    def parts_of(ref, rows, pair):
        return [ref[rows, lanes_of(pair, part)] for part in range(3)]

    def slot_rows(s):
        return slice(s * short_length, (s + 1) * short_length)

    long_rows = slice(seg_rows, 2 * seg_rows)

    def attend_long():
        position = lax.broadcasted_iota(jnp.int32, (1, long_length), 1)
        bias = jnp.where(position < long_len, 0.0, NEGATIVE)
        for pair in range(pairs):
            qp, kp, vp = parts_of(r.qkv, long_rows, pair)
            parts = []
            for j, pick in enumerate((first, second)):
                (probs,) = softmax([mm_nt(pick(qp), kp) + bias])
                r.pl[2 * pair + j] = probs
                parts.append(mm(probs, vp))
            r.ctx[long_rows, lanes_of(pair)] = jnp.where(low_lane, *parts).astype(BF)

    def attend_short():
        position = lax.broadcasted_iota(jnp.int32, (1, short_length), 1)
        scores = []
        for s in range(short_slots):
            bias = jnp.where(position < short_len(s), 0.0, NEGATIVE)
            for pair in range(pairs):
                qp, kp, _ = parts_of(r.qkv, slot_rows(s), pair)
                scores += [mm_nt(first(qp), kp) + bias, mm_nt(second(qp), kp) + bias]
        probs = softmax(scores)
        for s in range(short_slots):
            for pair in range(pairs):
                parts = []
                for head in (2 * pair, 2 * pair + 1):
                    r.ps[s, head] = probs[s * heads + head]
                    parts.append(mm(probs[s * heads + head], r.qkv[slot_rows(s), lanes_of(pair, 2)]))
                r.ctx[slot_rows(s), lanes_of(pair)] = jnp.where(low_lane, *parts).astype(BF)

    def exchange(stage, seg, left, right, product, between=lambda: None):
        index = 2 * stage + seg
        r.out_buf[index] = product(left[rows_of(peer_start(seg), half), :], right[...]).astype(BF)
        cp = remote(r.out_buf.at[index], r.in_buf.at[index], index, peer)
        between()
        r.own[seg] = product(left[rows_of(own_start(seg), half), :], right[...])
        return cp

    def share(index, seg, ref):
        rows = rows_of(own_start(seg), half)
        return remote(ref.at[rows], ref.at[rows], index, peer)

    def norm(values):
        mean = jnp.mean(values, axis=-1, keepdims=True)
        centred = values - mean
        scale = lax.rsqrt(jnp.mean(centred * centred, axis=-1, keepdims=True) + EPSILON)
        return centred * scale, scale

    def norm_back(normed, scale, grad):
        return scale * (
            grad
            - jnp.mean(grad, axis=-1, keepdims=True)
            - normed * jnp.mean(grad * normed, axis=-1, keepdims=True)
        )

    def norm_one(seg):
        for t in range(half // tile):
            mine = slice(seg * half + t * tile, seg * half + (t + 1) * tile)
            here = slice(t * tile, (t + 1) * tile)
            rows = rows_of(own_start(seg) + t * tile, tile)
            total = r.own[seg, here, :] + r.in_buf[seg, here, :].astype(F32) + ob
            normed, scale = norm(r.x[rows, :].astype(F32) + total)
            r.n1[mine, :] = normed
            r.r1[mine, :] = scale
            r.h[rows, :] = (normed * g1 + b1).astype(BF)

    def up(start):
        rows = rows_of(start, half)
        step = 256
        for j in range(hidden // step):
            cols = slice(j * step, (j + 1) * step)
            pre = mm(r.h[rows, :], r.wu[:, cols]) + ub[:, cols]
            phi = 0.5 + 0.5 * lax.erf(pre * (0.5**0.5))
            r.f[rows, cols] = (pre * phi).astype(BF)
            r.gp[rows, cols] = (phi + pre * (jnp.exp(pre * pre * -0.5) * 0.3989422804014327)).astype(BF)

    def norm_two(seg):
        for t in range(half // tile):
            mine = slice(seg * half + t * tile, seg * half + (t + 1) * tile)
            here = slice(t * tile, (t + 1) * tile)
            rows = rows_of(own_start(seg) + t * tile, tile)
            row = lax.broadcasted_iota(jnp.int32, (tile, 1), 0)
            if seg == 0:
                slot, inner = t * tile // short_length, t * tile % short_length
                keep = row + inner < short_len(mp * (short_slots // 2) + slot)
                upstream = r.ups[slot, inner : inner + tile, :]
            else:
                keep = row + (mp * half + t * tile) < long_len
                upstream = r.upl[here, :]
            keep = keep.astype(F32)
            hidden_state = r.n1[mine, :] * g1 + b1
            total = r.own[seg, here, :] + r.in_buf[2 + seg, here, :].astype(F32) + db
            normed, scale = norm(hidden_state + total)
            r.out[seg, here, :] = (keep * (normed * g2 + b2)).astype(BF)
            grad = keep * upstream.astype(F32)
            r.acc[0] += fold(grad * normed)
            r.acc[1] += fold(grad)
            dsecond = norm_back(normed, scale, grad * g2)
            low = dsecond.astype(BF)
            r.acc[2] += fold(low.astype(F32))
            r.ds[mine, :] = dsecond
            r.do[rows, :] = low

    def norm_one_back(seg):
        for t in range(half // tile):
            mine = slice(seg * half + t * tile, seg * half + (t + 1) * tile)
            here = slice(t * tile, (t + 1) * tile)
            rows = rows_of(own_start(seg) + t * tile, tile)
            grad = r.ds[mine, :] + r.own[seg, here, :] + r.in_buf[4 + seg, here, :].astype(F32)
            normed = r.n1[mine, :]
            r.acc[3] += fold(grad * normed)
            r.acc[4] += fold(grad)
            dfirst = norm_back(normed, r.r1[mine, :], grad * g1)
            low = dfirst.astype(BF)
            r.acc[5] += fold(low.astype(F32))
            r.ds[mine, :] = dfirst
            r.da[rows, :] = low

    def active_back(seg):
        for part in range(2):
            rows = slice(seg * seg_rows + part * half, seg * seg_rows + (part + 1) * half)
            step = 512
            for j in range(hidden // step):
                cols = slice(j * step, (j + 1) * step)
                low = (mm_nt(r.do[rows, :], r.wd[cols, :]) * r.gp[rows, cols].astype(F32)).astype(BF)
                r.acc_up[:, cols] += fold(low.astype(F32))
                r.gp[rows, cols] = low
                yield

    def dscores(rows, pair, probs):
        vp, dc = r.qkv[rows, lanes_of(pair, 2)], r.dctx[rows, lanes_of(pair)]
        product = dc.astype(F32) * r.ctx[rows, lanes_of(pair)].astype(F32)
        held = []
        for j, pick in enumerate((first, second)):
            inner = jnp.sum(pick(product), axis=-1, keepdims=True)
            held.append((probs[j].astype(F32) * (mm_nt(pick(dc), vp) - inner)).astype(BF))
        return held

    def heads_back(rows, pair, probs, held):
        qp, kp, _ = parts_of(r.qkv, rows, pair)
        dc = r.dctx[rows, lanes_of(pair)]
        dq = jnp.where(low_lane, mm(held[0], kp), mm(held[1], kp)) * HEAD**-0.5
        r.dqkv[rows, lanes_of(pair)] = dq.astype(BF)
        r.dqkv[rows, lanes_of(pair, 1)] = jnp.where(low_lane, mm_tn(held[0], qp), mm_tn(held[1], qp)).astype(BF)
        r.dqkv[rows, lanes_of(pair, 2)] = jnp.where(low_lane, mm_tn(probs[0], dc), mm_tn(probs[1], dc)).astype(BF)

    def attend_long_back(pair):
        probs = [r.pl[2 * pair], r.pl[2 * pair + 1]]
        heads_back(long_rows, pair, probs, dscores(long_rows, pair, probs))

    def attend_short_back():
        each = [(s, pair) for s in range(short_slots) for pair in range(pairs)]
        probs = [[r.ps[s, 2 * pair], r.ps[s, 2 * pair + 1]] for s, pair in each]
        held = [dscores(slot_rows(s), pair, p) for (s, pair), p in zip(each, probs)]
        for (s, pair), p, h in zip(each, probs, held):
            heads_back(slot_rows(s), pair, p, h)

    begin, flight = {}, {}

    def half_copy(c, p):
        n = 8 >> p
        bit = ORDERS[KINDS[c]][p]
        start = begin.get(c, 0)
        held, landed = getattr(r, f"G{c}"), getattr(r, f"R{c}")
        cp = pltpu.make_async_remote_copy(
            src_ref=held.at[pl.ds(start + (1 - my_bit[bit]) * n, n)],
            dst_ref=landed.at[pl.ds(PARTS_AT[p], n)],
            send_sem=r.rs_send.at[c, p],
            recv_sem=r.rs_recv.at[c, p],
            device_id=across[bit],
            device_id_type=MESH,
        )
        cp.start()
        sends.append(cp)
        begin[c] = start + my_bit[bit] * n
        flight[c] = (p, cp)

    def operands(start, stop):
        for left, right in ((r.do, r.f), (r.h, r.gp), (r.da, r.ctx), (r.x, r.dqkv)):
            span = right.shape[1]
            if start < span:
                return left, right, slice(start, stop)
            start, stop = start - span, stop - span

    def gradient(begins, ends):
        blocks = 1 << BITS
        part = width // 2
        base = COLUMNS[begins]
        left, right, cols = operands(base, COLUMNS[ends])
        orders = [ORDERS[KINDS[c]] if reduce_here else (3, 2, 1, 0) for c in range(begins, ends)]

        @pl.loop(0, 2)
        def _(m):
            piece = mm_tn(left[:, rows_of(m * part, part)], right[:, cols]).astype(BF)
            for c, order in zip(range(begins, ends), orders):
                held = getattr(r, f"G{c}")
                own = piece[:, COLUMNS[c] - base : COLUMNS[c + 1] - base]
                for b in range(blocks // 2):
                    held[place(order, b) + m * place(order, blocks // 2)] = own[b * block : (b + 1) * block]

        if reduce_here:
            for c in range(begins, ends):
                half_copy(c, 0)

    vector = [None, 0]

    def vector_copy(k):
        r.vec_out[k] = r.vec[...].astype(BF)
        device = peer if k == 0 else across[k - 1]
        vector[:] = remote(r.vec_out.at[k], r.vec_in.at[k], 22 + k, device), k

    def vector_advance():
        cp, k = vector
        cp.wait_recv()
        rows = slice(8 if k == 0 else 0, 16)
        r.vec[rows, :] = (r.vec_out[k].astype(F32) + r.vec_in[k].astype(F32))[rows]
        if k < BITS and reduce_here:
            vector_copy(k + 1)
        else:
            cp = pltpu.make_async_copy(r.vec, r.sums, r.out_sem.at[7])
            cp.start()
            outs.append(cp)

    def advance(c):
        p, cp = flight.pop(c)
        n = 8 >> p
        held, landed = getattr(r, f"G{c}"), getattr(r, f"R{c}")
        cp.wait_recv()
        if p < BITS - 1:
            mine = pl.ds(begin[c], n)
            held[mine] = held[mine] + landed[PARTS_AT[p] : PARTS_AT[p] + n]
            half_copy(c, p + 1)
        else:
            total = held[begin[c]].astype(F32) + landed[PARTS_AT[p]].astype(F32)
            cols = slice(COLUMNS[c], COLUMNS[c + 1])
            r.held_rows[:, cols] = total
            cp = pltpu.make_async_copy(r.held_rows.at[:, cols], r.rows.at[:, cols], r.row_sem.at[c])
            cp.start()
            outs.append(cp)

    todo = list(EVENTS) if reduce_here else []
    marks = list(MARKS)

    def handle():
        c = todo.pop(0)
        if c < CHUNKS:
            advance(c)
        else:
            vector_advance()

    def point():
        upto = marks.pop(0) if marks else len(EVENTS)
        while todo and len(EVENTS) - len(todo) < upto:
            handle()

    def gradients(group):
        for job, begins, ends in JOBS:
            if job == group:
                point()
                gradient(begins, ends)

    for name in ("xl", "w0", "w1", "w2"):
        loads[name].wait()
    load_rest()
    project(1)
    attend_long()
    for s in range(short_slots):
        loads[f"xs{s}"].wait()
    project(0)
    loads["wo"].wait()
    pl.semaphore_wait(barrier, len(partners))
    ex = {}
    ex["a1"] = exchange(0, 1, r.ctx, r.wo, mm)
    attend_short()
    ex["a1"].wait_recv()
    norm_one(1)
    ex["h1"] = share(8, 1, r.h)
    ex["a0"] = exchange(0, 0, r.ctx, r.wo, mm)
    loads["wu"].wait()
    loads["wd"].wait()
    up(own_start(1))
    ex["h1"].wait_recv()
    up(peer_start(1))
    ex["a0"].wait_recv()
    norm_one(0)
    ex["h0"] = share(9, 0, r.h)
    ex["o1"] = exchange(1, 1, r.f, r.wd, mm)
    up(own_start(0))
    ex["h0"].wait_recv()
    up(peer_start(0))
    ex["o0"] = exchange(1, 0, r.f, r.wd, mm)
    loads["us"].wait()
    loads["ul"].wait()
    outs, arrivals = [], []

    def publish(index, seg, short_ref, long_ref, held):
        if seg == 0:
            for s in range(short_slots // 2):
                piece = held.at[0, pl.ds(s * short_length, short_length)]
                target = short_ref.at[mp * (short_slots // 2) + s]
                cp = pltpu.make_async_copy(piece, target, r.out_sem.at[index + s])
                cp.start()
                outs.append(cp)
                arrivals.append(remote(piece, target, 16 + index + s, peer))
        else:
            target = long_ref.at[0, rows_of(mp * half, half)]
            cp = pltpu.make_async_copy(held.at[1], target, r.out_sem.at[index + 2])
            cp.start()
            outs.append(cp)
            arrivals.append(remote(held.at[1], target, 16 + index + 2, peer))

    for seg in (1, 0):
        ex[f"o{seg}"].wait_recv()
        norm_two(seg)
        ex[f"do{seg}"] = share(10 + seg, seg, r.do)
    ex["do1"].wait_recv()

    early, late = active_back(1), active_back(0)
    for _ in range(EARLY):
        next(early)
    ex["do0"].wait_recv()
    gradients("d")
    point()
    publish(0, 1, r.os, r.ol, r.out)
    publish(0, 0, r.os, r.ol, r.out)
    for pieces in (early, late):
        for _ in pieces:
            point()
    gradients("u")
    for seg in (1, 0):
        point()
        ex[f"dh{seg}"] = exchange(2, seg, r.gp, r.wu, mm_nt, point)
    for seg in (1, 0):
        point()
        ex[f"dh{seg}"].wait_recv()
        norm_one_back(seg)
        ex[f"da{seg}"] = share(12 + seg, seg, r.da)
    for seg in (1, 0):
        point()
        ex[f"da{seg}"].wait_recv()
        rows = slice(seg * seg_rows, (seg + 1) * seg_rows)
        r.dctx[rows, :] = mm_nt(r.da[rows, :], r.wo[...]).astype(BF)
    gradients("o")
    point()
    pl.loop(0, pairs)(attend_long_back)
    point()
    attend_short_back()
    gradients("q")
    point()
    for j in range(2):
        r.acc_qv[:, j * local : (j + 1) * local] = fold(r.dqkv[:, 2 * j * local : (2 * j + 1) * local].astype(F32))

    def total_of(values):
        return jnp.sum(values, axis=0, keepdims=True)

    r.vec[...] = jnp.zeros_like(r.vec)
    r.vec[0:1, :] = total_of(r.acc_qv[...])
    r.vec[1:2, :] = total_of(r.acc_up[:, :width])
    r.vec[2:3, :] = total_of(r.acc_up[:, width:])
    for j in range(6):
        r.vec[8 + j : 9 + j, :] = total_of(r.acc[j])
    vector_copy(0)

    def input_part(rows):
        return mm_nt(r.dqkv[rows, :], r.wqkv[...])

    for seg in (1, 0):
        index = 6 + seg
        point()
        r.out_buf[index] = input_part(rows_of(peer_start(seg), half)).astype(BF)
        ex[f"dx{seg}"] = remote(r.out_buf.at[index], r.in_buf.at[index], index, peer)
        point()
        r.own[seg] = input_part(rows_of(own_start(seg), half))
    for seg in (1, 0):
        point()
        ex[f"dx{seg}"].wait_recv()
        dfirst = r.ds[seg * half : (seg + 1) * half, :]
        r.dxo[seg] = (dfirst + r.own[seg] + r.in_buf[6 + seg].astype(F32)).astype(BF)
        publish(3, seg, r.dxs, r.dxl, r.dxo)
    if reduce_here:
        while todo:
            handle()
    else:
        for c in range(CHUNKS):
            cp = pltpu.make_async_copy(
                getattr(r, f"G{c}"), r.grads.at[:, :, pl.ds(COLUMNS[c], COLUMNS[c + 1] - COLUMNS[c])], r.out_sem.at[6]
            )
            cp.start()
            cp.wait()
        vector_advance()

    for cp in outs:
        cp.wait()
    for cp in arrivals:
        cp.wait_recv()
    for cp in sends:
        cp.wait_send()


COLUMNS = (
    0, 128, 256, 384, 512, 768, 1024, 1280, 1536, 1792, 2048, 2304, 2560, 2816, 3072, 3328, 3456, 3712, 3968,
    4224, 4352, 4480, 4608,
)
KINDS = (
    14, 3, 16, 11, 7, 3, 4, 9, 5, 9, 0, 2, 6, 6, 9, 14, 1, 8, 0, 2, 0, 6,
)
CHUNKS = len(KINDS)
JOBS = (
    ("d", 0, 2),
    ("d", 2, 4),
    ("d", 4, 6),
    ("d", 6, 8),
    ("u", 8, 10),
    ("u", 10, 12),
    ("u", 12, 14),
    ("o", 14, 16),
    ("q", 16, 22),
)
EVENTS = (
    1, 3, 2, 5, 1, 3, 6, 7, 5, 9, 8, 4, 7, 12, 11, 10, 9, 13, 8, 4, 14, 12, 10, 14, 17, 16, 12, 0, 13, 18, 10,
    4, 16, 11, 17, 19, 8, 22, 13, 15, 21, 18, 20, 9, 11, 14, 19, 16, 2, 22, 17, 0, 1, 21, 15, 6, 18, 7, 20, 5,
    3, 19, 2, 22, 0, 21, 15, 20, 22, 6, 12, 4, 10, 8, 13, 9, 14, 16, 11, 1, 17, 7, 3, 5, 18, 2, 19, 0, 21, 15,
    20, 6, 22,
)
MARKS = (
    0, 0, 0, 0, 0, 0, 0, 1, 2, 2, 3, 3, 3, 3, 4, 4, 6, 7, 7, 8, 8, 9, 10, 10, 10, 11, 13, 15, 19, 20, 21, 21,
    21, 22, 23, 23,
)
EARLY = 3


def shards(n_dp, *args):
    (
        xs, xl, wq, qb, wk, wv, vb, wo, ob, g1, b1, wu, ub, wd, db, g2, b2, us, ul, sl, ll, live,
    ) = args
    short_slots, short_length, width = xs.shape
    long_length = xl.shape[1]
    local, hidden = wq.shape[1], wu.shape[1]
    heads = local // HEAD
    rows = short_slots * short_length + xl.shape[0] * long_length
    half = long_length // 2
    reduce_here = n_dp == 1 << BITS
    blocks = 1 << BITS
    block = width // blocks
    columns = 4 * local + 2 * hidden
    spans = [COLUMNS[c + 1] - COLUMNS[c] for c in range(CHUNKS)]
    assert COLUMNS[-1] == columns
    any_spec = pl.BlockSpec(memory_space=pl.ANY)
    vmem = pl.BlockSpec(memory_space=pltpu.VMEM)
    smem = pl.BlockSpec(memory_space=pltpu.SMEM)
    inputs = [
        ("sl", sl, smem), ("ll", ll, smem), ("live", live, smem),
        ("xs", xs, any_spec), ("xl", xl, any_spec), ("us", us, any_spec), ("ul", ul, any_spec),
        ("wq_h", wq, any_spec), ("wk_h", wk, any_spec), ("wv_h", wv, any_spec), ("wo_h", wo, any_spec),
        ("wu_h", wu, any_spec), ("wd_h", wd, any_spec),
        ("qb", qb, vmem), ("vb", vb, vmem), ("ob", ob, vmem), ("g1", g1, vmem), ("b1", b1, vmem),
        ("ub", ub, vmem), ("db", db, vmem), ("g2", g2, vmem), ("b2", b2, vmem),
    ]
    sds = jax.ShapeDtypeStruct
    outputs = [
        ("os", sds(xs.shape, BF), any_spec), ("ol", sds(xl.shape, BF), any_spec),
        ("dxs", sds(xs.shape, BF), any_spec), ("dxl", sds(xl.shape, BF), any_spec),
    ]
    if reduce_here:
        outputs.append(("rows", sds((block, columns), F32), any_spec))
    else:
        outputs.append(("grads", sds((blocks, block, columns), BF), any_spec))
    outputs.append(("sums", sds((16, width), F32), any_spec))
    v = pltpu.VMEM
    dma = pltpu.SemaphoreType.DMA
    scratch = [
        ("x", v((rows, width), BF)), ("ups", v((short_slots // 2, short_length, width), BF)), ("upl", v((half, width), BF)),
        ("wqkv", v((width, 3 * local), BF)), ("wo", v(wo.shape, BF)),
        ("wu", v(wu.shape, BF)), ("wd", v(wd.shape, BF)),
        ("qkv", v((rows, 3 * local), BF)),
        ("pl", v((heads, long_length, long_length), BF)), ("ps", v((short_slots, heads, short_length, short_length), BF)),
        ("ctx", v((rows, local), BF)), ("n1", v((2 * half, width), F32)), ("r1", v((2 * half, 1), F32)),
        ("h", v((rows, width), BF)), ("f", v((rows, hidden), BF)), ("gp", v((rows, hidden), BF)),
        ("do", v((rows, width), BF)), ("ds", v((2 * half, width), F32)), ("da", v((rows, width), BF)),
        ("dctx", v((rows, local), BF)), ("dqkv", v((rows, 3 * local), BF)),
        ("own", v((2, half, width), F32)), ("out_buf", v((8, half, width), BF)), ("in_buf", v((8, half, width), BF)),
        ("out", v((2, half, width), BF)), ("dxo", v((2, half, width), BF)),
        ("acc", v((6, 8, width), F32)), ("acc_up", v((8, hidden), F32)), ("acc_qv", v((8, 2 * local), F32)),
        ("vec", v((16, width), F32)), ("vec_out", v((5, 16, width), BF)), ("vec_in", v((5, 16, width), BF)),
        ("load_sem", dma((16,))), ("out_sem", dma((8,))), ("ex_send", dma((28,))), ("ex_recv", dma((28,))),
        ("held_rows", v((block, columns), F32)), ("row_sem", dma((len(spans),))),
        ("rs_send", dma((len(spans), BITS))), ("rs_recv", dma((len(spans), BITS))),
    ]
    for c, span in enumerate(spans):
        scratch.append((f"G{c}", v((blocks, block, span), BF)))
        scratch.append((f"R{c}", v((blocks - 1 if reduce_here else 1, block, span), BF)))
    names = [n for n, *_ in inputs] + [n for n, *_ in outputs] + [n for n, *_ in scratch]
    macs = rows * width * (8 * local + 6 * hidden)
    results = pl.pallas_call(
        functools.partial(layer, reduce_here, names),
        out_shape=[o[1] for o in outputs],
        in_specs=[i[2] for i in inputs],
        out_specs=[o[2] for o in outputs],
        scratch_shapes=[s[1] for s in scratch],
        cost_estimate=pl.CostEstimate(flops=2 * macs, bytes_accessed=20 << 20, transcendentals=0),
        compiler_params=pltpu.CompilerParams(
            collective_id=0, has_side_effects=True, vmem_limit_bytes=62 << 20
        ),
    )(*[i[1] for i in inputs])
    got = dict(zip([o[0] for o in outputs], results, strict=True))
    if not reduce_here:
        grads = got["grads"].reshape(width, columns).astype(F32)
        got["rows"] = lax.psum_scatter(grads, "dp", scatter_dimension=0, tiled=True)
        got["sums"] = lax.psum(got["sums"], "dp")
    block = width // n_dp
    finals = [
        ("os", sds(xs.shape, BF), any_spec), ("ol", sds(xl.shape, BF), any_spec),
        ("dxs", sds(xs.shape, BF), any_spec), ("dxl", sds(xl.shape, BF), any_spec),
        ("gq", sds((block, local), F32), any_spec), ("g_qb", sds((local // n_dp,), F32), vmem),
        ("gk", sds((block, local), F32), any_spec), ("gv", sds((block, local), F32), any_spec),
        ("g_vb", sds((local // n_dp,), F32), vmem), ("gout", sds((block, local), F32), any_spec),
        ("g_ob", sds((block,), F32), vmem), ("g_gain1", sds((block,), F32), vmem), ("g_shift1", sds((block,), F32), vmem),
        ("gup", sds((block, hidden), F32), any_spec), ("g_ub", sds((hidden // n_dp,), F32), vmem),
        ("gdown", sds((block, hidden), F32), any_spec),
        ("g_db", sds((block,), F32), vmem), ("g_gain2", sds((block,), F32), vmem), ("g_shift2", sds((block,), F32), vmem),
    ]
    sources = ("os", "ol", "dxs", "dxl", "rows", "sums")
    names = ["in_" + n for n in sources] + [f[0] for f in finals] + ["held_" + n for n in sources] + ["into", "out"]
    results = pl.pallas_call(
        functools.partial(place_results, n_dp, names),
        out_shape=[f[1] for f in finals],
        in_specs=[any_spec] * 6,
        out_specs=[f[2] for f in finals],
        scratch_shapes=[v(got[n].shape, got[n].dtype) for n in sources] + [dma((11,)), dma((10,))],
        cost_estimate=pl.CostEstimate(flops=0, bytes_accessed=8 << 20, transcendentals=0),
        compiler_params=pltpu.CompilerParams(vmem_limit_bytes=62 << 20),
    )(*[got[n] for n in sources])
    return tuple(result.T if f[0] in ("gout", "gdown") else result for f, result in zip(finals, results, strict=True))


def place_results(n_dp, names, *refs):
    r = Refs()
    for name, ref in zip(names, refs, strict=True):
        setattr(r, name, ref)
    moves = [(getattr(r, "in_" + n), getattr(r, "held_" + n), getattr(r, n)) for n in ("os", "ol", "dxs", "dxl")]
    at = 0
    for ref in (r.gdown, r.gup, r.gout, r.gq, r.gk, r.gv):
        cols = slice(at, at + ref.shape[1])
        moves.append((r.in_rows.at[:, cols], r.held_rows.at[:, cols], ref))
        at += ref.shape[1]
    into = [pltpu.make_async_copy(source, held, r.into.at[j]) for j, (source, held, _) in enumerate(moves)]
    out = [pltpu.make_async_copy(held, target, r.out.at[j]) for j, (_, held, target) in enumerate(moves)]
    vectors = pltpu.make_async_copy(r.in_sums, r.held_sums, r.into.at[10])
    vectors.start()
    for cp in into:
        cp.start()
    vectors.wait()
    vector_results(r)
    for cp, back in zip(into, out):
        cp.wait()
        back.start()
    for cp in out:
        cp.wait()


def vector_results(r):
    dp = lax.axis_index("dp")
    local = r.gq.shape[1]
    width = r.held_sums.shape[1]

    def turn(start):
        return pltpu.roll(r.held_sums[...], lax.rem(2 * width - start, width), 1)

    size = r.g_ob.shape[0]
    turned = turn(dp * size)
    for j, ref in enumerate((r.g_gain2, r.g_shift2, r.g_db, r.g_gain1, r.g_shift1, r.g_ob)):
        ref[...] = turned[8 + j : 9 + j, :size].reshape(size)
    size = r.g_qb.shape[0]
    turned = turn(dp * size)
    r.g_qb[...] = turned[0:1, :size].reshape(size)
    r.g_vb[...] = turned[0:1, local : local + size].reshape(size)
    size = r.g_ub.shape[0]
    turned = turn(lax.rem(dp * size, width))
    r.g_ub[...] = jnp.where(dp * size < width, turned[1:2, :size], turned[2:3, :size]).reshape(size)


def solution(mesh):
    in_specs = (
        P("dp", None, None), P("dp", None, None), P(None, "mp"), P("mp"), P(None, "mp"), P(None, "mp"), P("mp"),
        P("mp", None), P(), P(), P(), P(None, "mp"), P("mp"), P("mp", None), P(), P(), P(),
        P("dp", None, None), P("dp", None, None), P("dp"), P("dp"), P("dp", None),
    )
    out_specs = (
        P("dp", None, None), P("dp", None, None), P("dp", None, None), P("dp", None, None),
        P("dp", "mp"), P(("mp", "dp")), P("dp", "mp"), P("dp", "mp"), P(("mp", "dp")), P("mp", "dp"),
        P("dp"), P("dp"), P("dp"), P("dp", "mp"), P(("mp", "dp")), P("mp", "dp"), P("dp"), P("dp"), P("dp"),
    )
    return jax.shard_map(
        functools.partial(shards, mesh.shape["dp"]),
        mesh=mesh, in_specs=in_specs, out_specs=out_specs, check_vma=False,
    )
```
